32 devices in a mesh: tm: 8 (over y, x, core), chan: 4 (over z).
Axes of the slice: x: 2, y: 2, z: 4, core: 2. Of those that a mesh axis runs over, the one named last changes fastest.
Arguments:
- latents: bfloat16 [512, 32, 512], P('chan', 'tm'), may hold values from -6 to 6
- conv_weight: bfloat16 [512, 3, 9, 512], P(None, None, None, 'chan'), may hold values from -0.0546875 to 0.0546875
- norm_gain: float32 [512], P('chan'), may hold values from 0.1 to 1.9
- norm_bias: float32 [512], P('chan'), may hold values from -3 to 3
- clip_lengths: int32 [12], replicated, may hold values from 1 to 8, 32 in all
- slab_bounds: int32 [8, 2], P('tm'), may hold values from 0 to 32, as said below
Outputs:
- decoded: bfloat16 [512, 64, 512], P('chan', 'tm')
The draws below stay inside these ranges and needn't reach their ends.
Inputs may be any that keep to these rules, and one draw needn't show every extreme that they name: `clip_lengths`: the clips lie end to end and cover all 32 frames; the longest clip has exactly a quarter of 32 frames. `slab_bounds`: slab 0 starts at frame 0, the last slab ends at 32, each slab ends where the next starts, slab s starts within 2 frames of s * 4, so a slab holds 0 to 8 frames; some slab holds exactly 8 frames.
All inputs are finite; a program needn't handle non-finite values.
Results may differ from the reference program's by a relative error of at most 0.001.
Values may be sent and summed in bfloat16 or wider, within the bound.
No kernel may reach another device: no remote copies, remote signals or barrier semaphores. Data moves between devices by JAX's collectives and lax.ppermute only.
A program may use at most 128 MiB of HBM per device.

```python
import math
import jax
import jax.numpy as jnp
import numpy as np
from jax import lax

C = 512
GROUPS = 32
FR_DEV = 4
H = 16
W = 32
NCLIP = 12
FRAMES = 32
CAP = 8
N_TM = 8


def draw_slab_bounds(key, part):
    key = jax.random.fold_in(key, 7)
    half_slab = FR_DEV // 2
    shifts = jax.random.randint(key, (N_TM + 1,), -half_slab, half_slab + 1)
    picked = jax.random.randint(jax.random.fold_in(key, 1), (), 1, N_TM - 2)
    position = jnp.arange(N_TM + 1)
    shifts = jnp.where(position == picked, -half_slab, shifts)
    shifts = jnp.where(position == picked + 1, half_slab, shifts)
    shifts = jnp.where((position == 0) | (position == N_TM), 0, shifts)
    starts = position * FR_DEV + shifts
    return jnp.stack([starts[:-1], starts[1:]], axis=1).astype(jnp.int32)


def block_levels(rng, dims, cuts, least, top_value):
    loudness, own = 1.0, jax.random.fold_in(rng, 6)
    for axis_at, blocks in cuts:
        heights = jnp.exp(jax.random.uniform(jax.random.fold_in(own, axis_at), (blocks,), jnp.float32, least / len(cuts), top_value / len(cuts)))
        loudness = loudness * jnp.repeat(heights, dims[axis_at] // blocks).reshape([-1 if axis == axis_at else 1 for axis in range(len(dims))])
    return loudness


def split_up(amount, total, reach, lean):
    weights = [(1 << 20) // math.isqrt(grade ** lean) + 1 for grade in range(2, amount + 1)]
    spare, holding = total - reach - (amount - 1), [1] * (amount - 1)
    while spare > 0:
        candidates = [i for i in range(amount - 1) if holding[i] < reach]
        pool, budget = sum([weights[i] for i in candidates]), spare
        for i in candidates:
            more = min(reach - holding[i], max(1, budget * weights[i] // pool), spare)
            holding[i] = holding[i] + more
            spare = spare - more
    return np.array([reach] + holding)


def uneven_parts(own_key, amount, total, most, skew):
    if amount == 2:
        one = jax.random.randint(own_key, (), max(1, total - most), min(most, total - 1) + 1)
        return jnp.stack([one, total - one])
    tallies = jnp.asarray(split_up(amount, total, most, skew), jnp.int32)
    pairs = (amount - 1) // 2
    giver, sink = tallies[1:1 + 2 * pairs:2], tallies[2:2 + 2 * pairs:2]
    margin = jnp.minimum(giver - 1, most - sink)
    moved = jax.random.randint(jax.random.fold_in(own_key, 1), (pairs,), 0, 1 << 20) % (margin + 1)
    tallies = tallies.at[1:1 + 2 * pairs:2].set(giver - moved).at[2:2 + 2 * pairs:2].set(sink + moved)
    return tallies[jax.random.permutation(jax.random.fold_in(own_key, 2), amount)]


def bell_draw(key, extent, scale, reach, split=(), dtype=jnp.bfloat16):
    level = block_levels(key, extent, split, -0.22, 0.18) if split else 1.0
    entries = jax.random.normal(key, extent, jnp.float32) * scale * level
    return jnp.minimum(jnp.maximum(entries, -reach), reach).astype(dtype)


def setup_inputs(seed: int = 0) -> dict:
    splits = jax.random.split(jax.random.key(seed), 7)
    return {
        "latents": bell_draw(splits[0], (C, FRAMES, H * W), 1.0, 6.0, ((0, 4), (1, 8))),
        "conv_weight": bell_draw(splits[1], (C, 3, 9, C), (27 * C) ** -0.5, 0.0546875, ((3, 4),)),
        "norm_gain": jnp.clip(1.0 + 0.18 * jax.random.normal(splits[2], (C,), jnp.float32), 0.1, 1.9),
        "norm_bias": bell_draw(splits[3], (C,), 0.5, 3.0, ((0, 4),), jnp.float32),
        "clip_lengths": uneven_parts(splits[4], NCLIP, FRAMES, FRAMES // 4, 2).astype(jnp.int32),
        "slab_bounds": draw_slab_bounds(jax.random.fold_in(splits[6], 71), 0),
    }


norm_eps = 1e-06

def frame_starts(clip_lengths, frames):
    clip_ends = jnp.cumsum(clip_lengths)
    starts = clip_ends - clip_lengths
    chosen = jnp.where(starts[None, :] <= frames[:, None], starts[None, :], 0)
    return lax.optimization_barrier(jnp.max(chosen, axis=1)).astype(jnp.int32)

def tap_sources(frames, clip_lengths):
    clip_first = frame_starts(clip_lengths, frames)
    return jnp.stack([jnp.maximum(frames - 2 + offset, clip_first) for offset in range(3)]).astype(jnp.int32)

def columns(extended, local_index):
    channels = extended.shape[0]
    frame_count = local_index.shape[0]
    picked = jnp.take(extended, local_index.astype(jnp.int32), axis=1).reshape(channels, frame_count, H, W)
    padded = jnp.pad(picked, ((0, 0), (0, 0), (1, 1), (1, 1)))
    pieces = [padded[:, :, row_tap:row_tap + H, col_tap:col_tap + W] for row_tap in range(3) for col_tap in range(3)]
    return jnp.stack(pieces).reshape(9 * channels, frame_count * H * W)

def norm_block(summed, residual, norm_gain, norm_bias):
    channels, frame_count, cell_count = summed.shape
    group_width = C // GROUPS
    grouped = summed.reshape(channels // group_width, group_width, frame_count, cell_count)
    average = lax.optimization_barrier(jnp.mean(grouped, axis=(1, 3), keepdims=True))
    variance = lax.optimization_barrier(jnp.mean(jnp.square(grouped - average), axis=(1, 3), keepdims=True))
    normed = ((grouped - average) * lax.rsqrt(variance + norm_eps)).reshape(channels, frame_count, cell_count)
    normed = normed * norm_gain[:, None, None] + norm_bias[:, None, None]
    return (jax.nn.silu(normed) + residual.astype(jnp.float32)).astype(jnp.bfloat16)

def reference(latents, conv_weight, norm_gain, norm_bias, clip_lengths, slab_bounds):
    channels = latents.shape[0]
    weights = [conv_weight[:, offset].reshape(channels, 9 * channels) for offset in range(3)]

    def one_block(block_index):
        frames = (block_index * FR_DEV + jnp.arange(FR_DEV)).astype(jnp.int32)
        sources = tap_sources(frames, clip_lengths)
        summed = jnp.zeros((channels, FR_DEV * H * W), jnp.float32)
        for offset in range(3):
            summed = summed + jnp.dot(weights[offset], columns(latents, sources[offset]), preferred_element_type=jnp.float32)
        residual = jnp.take(latents, frames, axis=1)
        return norm_block(summed.reshape(channels, FR_DEV, H * W), residual, norm_gain, norm_bias)
    blocks = lax.map(one_block, jnp.arange(N_TM).astype(jnp.int32))
    decoded_full = jnp.transpose(blocks, (1, 0, 2, 3)).reshape(channels, FRAMES, H * W)
    slot_index = jnp.arange(CAP).astype(jnp.int32)
    slab_first = slab_bounds[:, 0]
    slab_sizes = slab_bounds[:, 1] - slab_first
    occupied = slot_index[None, :] < slab_sizes[:, None]
    wanted = jnp.where(occupied, slab_first[:, None] + slot_index[None, :], slab_first[:, None]).astype(jnp.int32)
    picked = jnp.take(decoded_full, wanted.reshape(-1), axis=1)
    return jnp.where(occupied.reshape(-1)[None, :, None], picked, jnp.zeros_like(picked))
```

```python
import functools

import jax
import jax.numpy as jnp
from jax import lax
from jax.experimental import pallas as pl
from jax.experimental.pallas import tpu as pltpu
from jax.sharding import PartitionSpec as P

C = 512
GROUPS = 32
H = 16
W = 32
CELLS = H * W
GROUP_WIDTH = C // GROUPS
PIECES = 8
TAPS = 27
LANES = 128
VMEM_BYTES = 9 * 1024 * 1024

norm_eps = 1e-06


def clip_start(clip_ref, g):
    first = jnp.int32(0)
    running = jnp.int32(0)
    for c in range(clip_ref.shape[0]):
        first = jnp.where(running <= g, jnp.maximum(first, running), first)
        running = running + clip_ref[c]
    return first


def group_sum(grouped):
    tiles = [grouped[:, :, i : i + LANES] for i in range(0, CELLS, LANES)]
    while len(tiles) > 1:
        tiles = [x + y for x, y in zip(tiles[::2], tiles[1::2])]
    folded = tiles[0][:, :8] + tiles[0][:, 8:]
    return jnp.sum(jnp.sum(folded, axis=1, keepdims=True), axis=2, keepdims=True)


def group_norm(total, gain, bias):
    own = total.shape[0]
    grouped = total.reshape(own // GROUP_WIDTH, GROUP_WIDTH, CELLS)
    scale = 1.0 / (GROUP_WIDTH * CELLS)
    centred = grouped - group_sum(grouped) * scale
    variance = group_sum(centred * centred) * scale
    normed = (centred * lax.rsqrt(variance + norm_eps)).reshape(own, CELLS)
    return normed * gain + bias


def as_column(row):
    count = row.shape[1]
    return jnp.transpose(jnp.broadcast_to(row, (count, count)))[:, :1]


def finished(total, gain, bias, residual):
    normed = group_norm(total, gain, bias)
    activated = normed / (1.0 + jnp.exp(-normed))
    return (activated + residual.astype(jnp.float32)).astype(jnp.bfloat16)


def conv_kernel(parts, halo, slots_of, groups, added, finish, ordered, *refs):
    refs = list(refs)
    clip_ref = refs.pop(0)
    frame_refs = [refs.pop(0) for _ in range(parts)]
    halo_ref = refs.pop(0) if halo else None
    weight_refs = [refs.pop(0) for _ in range(1 if slots_of is None else PIECES)]
    sum_refs = [[refs.pop(0) for _ in range(count)] for count in added]
    if finish:
        residual_ref = refs.pop(0)
        gain, bias = [as_column(refs.pop(0)[...]) for _ in range(2)]
    out_refs = [refs.pop(0) for _ in groups]
    shifted_ref = refs.pop(0)
    total_ref = refs.pop(0) if finish else None
    frame_count, shard, _ = frame_refs[0].shape
    half, own, _ = out_refs[0].shape
    piece_rows = own // PIECES
    slab = lax.axis_index("tm")
    place = slab % PIECES
    first_frame = slab * frame_count

    def piece_start(i):
        return pl.multiple_of(jnp.bitwise_xor(place, i) * piece_rows, piece_rows)

    cell = lax.broadcasted_iota(jnp.int32, (1, CELLS), 1)
    column = cell % W
    for p in range(parts):
        needed = list(range(frame_count + (2 if halo else 0)))
        if groups == ("next",):
            needed = needed[half:]
        if groups == ("head",):
            needed = needed[:half] + needed[frame_count:]
        for f in needed:
            frame = frame_refs[p][f] if f < frame_count else halo_ref[f - frame_count]
            zero = jnp.zeros_like(frame)
            shifted_ref[p, f, 0:shard, :] = jnp.where(column > 0, pltpu.roll(frame, 1, 1), zero)
            shifted_ref[p, f, shard : 2 * shard, :] = frame
            shifted_ref[p, f, 2 * shard :, :] = jnp.where(
                column < W - 1, pltpu.roll(frame, CELLS - 1, 1), zero
            )
        if not halo:
            shifted_ref[p, frame_count] = jnp.zeros_like(shifted_ref[p, frame_count])

    def weight_rows(p, i):
        if slots_of is None:
            return weight_refs[0][:, pl.ds(piece_start(i), piece_rows), :]
        return weight_refs[i][slots_of[p]]

    def convolved(j, time_taps):
        g = first_frame + j
        first = clip_start(clip_ref, g)
        inputs = []
        for p in range(parts):
            for k in time_taps:
                source = jnp.maximum(g - 2 + k, first) - first_frame
                if halo:
                    source = jnp.where(source < 0, source + frame_count + 2, source)
                else:
                    source = jnp.where(source < 0, frame_count, jnp.minimum(source, frame_count))
                inputs.append(shifted_ref[p, source])
        pieces = [[weight_rows(p, i) for i in range(PIECES)] for p in range(parts)]
        weights = []
        for a in range(3):
            for block in range(PIECES):
                row = [
                    pieces[p][block][9 * k + 3 * a + b]
                    for p in range(parts)
                    for k in time_taps
                    for b in range(3)
                ]
                weights.append(jnp.concatenate(row, axis=1))
        product = jnp.dot(
            jnp.concatenate(weights, axis=0),
            jnp.concatenate(inputs, axis=0),
            preferred_element_type=jnp.float32,
        )
        up = pltpu.roll(product[:own], W, 1)
        down = pltpu.roll(product[2 * own :], CELLS - W, 1)
        return (
            jnp.where(cell >= W, up, 0.0)
            + product[own : 2 * own]
            + jnp.where(cell < CELLS - W, down, 0.0)
        )

    def store_in_order(ref, total):
        for block in range(PIECES):
            ref[pl.ds(piece_start(block), piece_rows), :] = total[
                block * piece_rows : (block + 1) * piece_rows
            ]

    for group, out_ref, earlier in zip(groups, out_refs, sum_refs):
        if group == "next":
            for i, time_taps in enumerate(((0, 1), (0,))):
                total = convolved(frame_count + i, time_taps)
                for sum_ref in earlier:
                    total = total + sum_ref[i]
                if group in ordered:
                    store_in_order(out_ref.at[i], total)
                else:
                    out_ref[i] = total
            continue

        def one_frame(i, carry, group=group, out_ref=out_ref, earlier=earlier):
            j = i if group == "head" else i + half
            total = convolved(j, (0, 1, 2))
            for sum_ref in earlier[:1]:
                total = total + sum_ref[i]
            if group in finish:
                store_in_order(total_ref, total)
                total = total_ref[...]
                for sum_ref in earlier[1:]:
                    total = total + sum_ref[i]
                out_ref[i] = finished(total, gain, bias, residual_ref[j])
            else:
                out_ref[i] = total
            return carry

        lax.fori_loop(0, half, one_frame, 0)


def conv_parts(clip_lengths, shards_in, halo, weights, slots_of, groups, added, params, finish, ordered):
    frame_count, shard, cells = shards_in[0].shape
    own, half, parts = shard, frame_count // 2, len(shards_in)
    vectors = pl.BlockSpec(memory_space=pltpu.VMEM)
    operands = [clip_lengths, *shards_in]
    if halo is not None:
        operands.append(halo)
    operands += list(weights)
    for sums in added:
        operands += list(sums)
    if finish:
        operands += list(params)
    frames = frame_count + (1 if halo is None else 2)
    scratch = [pltpu.VMEM((parts, frames, 3 * shard, cells), jnp.bfloat16)]
    if finish:
        scratch.append(pltpu.VMEM((own, cells), jnp.float32))
    kernel = functools.partial(
        conv_kernel,
        parts,
        halo is not None,
        slots_of,
        groups,
        [len(sums) for sums in added],
        finish,
        ordered,
    )
    return pl.pallas_call(
        kernel,
        out_shape=[
            jax.ShapeDtypeStruct(
                (half, own, cells), jnp.bfloat16 if group in finish else jnp.float32
            )
            for group in groups
        ],
        in_specs=[pl.BlockSpec(memory_space=pltpu.SMEM)] + [vectors] * (len(operands) - 1),
        out_specs=[vectors] * len(groups),
        scratch_shapes=scratch,
        compiler_params=pltpu.CompilerParams(vmem_limit_bytes=VMEM_BYTES),
        cost_estimate=pl.CostEstimate(
            flops=2500000000 if groups == ("tail",) else 1024,
            bytes_accessed=1024,
            transcendentals=0,
        ),
        name="conv_parts",
    )(*operands)


def slots_kernel(bounds_ref, before_ref, head_ref, tail_ref, after_ref, out_ref, slot_ref):
    half, channels, _ = head_ref.shape
    capacity = out_ref.shape[1]
    offset = bounds_ref[0, 0] - (lax.axis_index("tm") * 2 * half - half)
    size = bounds_ref[0, 1] - bounds_ref[0, 0]
    for w in range(capacity):
        pair = (before_ref, head_ref, tail_ref, after_ref)[w // half]
        slot = w - offset

        @pl.when((slot >= 0) & (slot < size))
        def _():
            slot_ref[slot] = pair[w % half].astype(jnp.float32)

        @pl.when(w >= size)
        def _():
            slot_ref[w] = jnp.zeros_like(slot_ref[w])

    rows = 16
    for start in range(0, channels, rows):
        block = slot_ref[:, start : start + rows, :]
        out_ref[start : start + rows] = jnp.swapaxes(block, 0, 1).astype(jnp.bfloat16)


def slots(bounds, before, head, tail, after):
    half, channels, cells = head.shape
    capacity = 4 * half
    vectors = pl.BlockSpec(memory_space=pltpu.VMEM)
    return pl.pallas_call(
        slots_kernel,
        out_shape=jax.ShapeDtypeStruct((channels, capacity, cells), jnp.bfloat16),
        in_specs=[pl.BlockSpec(memory_space=pltpu.SMEM)] + [vectors] * 4,
        out_specs=vectors,
        scratch_shapes=[pltpu.VMEM((capacity, channels, cells), jnp.float32)],
        compiler_params=pltpu.CompilerParams(vmem_limit_bytes=VMEM_BYTES),
        name="slots",
    )(bounds, before, head, tail, after)


def xor_permute(array, axis, bits):
    return lax.ppermute(array, axis, [(i, i ^ bits) for i in range(lax.axis_size(axis))])


def weight_blocks(by_tap):
    _, out_channels, shard = by_tap.shape
    chan_count = lax.axis_size("chan")
    own = out_channels // chan_count
    piece_rows = own // PIECES
    piece = lax.axis_index("tm") % PIECES
    me = lax.axis_index("chan")
    pieces = [
        lax.dynamic_slice(
            by_tap,
            (0, jnp.bitwise_xor(me, s) * own + piece * piece_rows, 0),
            (TAPS, piece_rows, shard),
        )
        for s in range(1, chan_count)
    ]
    return lax.dynamic_slice(by_tap, (0, me * own, 0), (TAPS, own, shard)), pieces


def shards(latents, conv_weight, norm_gain, norm_bias, clip_lengths, slab_bounds):
    own, frame_count, cells = latents.shape
    out_channels, _, _, shard = conv_weight.shape
    tm_count = lax.axis_size("tm")
    forward = [(i, i + 1) for i in range(tm_count - 1)]
    backward = [(i + 1, i) for i in range(tm_count - 1)]

    by_tap = jnp.transpose(conv_weight, (1, 2, 0, 3)).reshape(TAPS, out_channels, shard)
    own_weights, blocks = weight_blocks(by_tap)
    blocks, latents = lax.optimization_barrier((blocks, latents))
    by_frame = jnp.transpose(latents, (1, 0, 2))
    swapped = [xor_permute(block, "chan", s) for s, block in enumerate(blocks, 1)]

    half = frame_count // 2

    def conv(shards_in, halo, given, slots_of, groups, added, params=(), finish=(), ordered=()):
        return conv_parts(
            clip_lengths, shards_in, halo, given, slots_of, groups, added, params, finish, ordered
        )

    swapped[0], by_frame = lax.optimization_barrier((swapped[0], by_frame))
    first = xor_permute(by_frame, "chan", 1)
    swapped, kept = lax.optimization_barrier((jnp.stack(swapped), by_frame))
    second = xor_permute(kept, "chan", 2)
    first, by_frame = lax.optimization_barrier((first, by_frame))
    totals = conv([by_frame], None, [own_weights], None, ("head", "tail", "next"), [[], [], []])
    same_core = [swapped] + [xor_permute(swapped, "tm", bits) for bits in range(2, PIECES, 2)]
    same_core, totals = lax.optimization_barrier((same_core, totals))
    head, tail, following = totals
    other_core = [xor_permute(piece, "tm", 1) for piece in same_core]
    weights = [piece for pair in zip(same_core, other_core) for piece in pair]
    third = xor_permute(second, "chan", 1)
    chan_count = lax.axis_size("chan")
    third_halo = lax.ppermute(
        second[half:],
        ("tm", "chan"),
        [
            (t * chan_count + (c ^ 1), (t + 1) * chan_count + c)
            for t in range(tm_count - 1)
            for c in range(chan_count)
        ],
    )
    pair, slots_of = [first, second], (0, 1)
    (following,) = conv(
        pair, None, weights, slots_of, ("next",), [[following]], ordered=("next",)
    )
    arrived = lax.ppermute(following, "tm", forward)
    both = ("head", "tail")
    head, tail = conv(pair, None, weights, slots_of, both, [[head], [tail]])
    params = (by_frame, norm_gain.reshape(1, own), norm_bias.reshape(1, own))
    (tail,) = conv([third], None, weights, (2,), ("tail",), [[tail]], params, ("tail",))
    before = lax.ppermute(tail, "tm", forward)
    arrived, tail = lax.optimization_barrier((arrived, tail))
    (head,) = conv(
        [third], third_halo, weights, (2,), ("head",), [[head, arrived]], params, ("head",)
    )
    after = lax.ppermute(head, "tm", backward)
    return slots(slab_bounds, before, head, tail, after)


def solution(mesh):
    placed = (
        P("chan", "tm", None),
        P(None, None, None, "chan"),
        P("chan"),
        P("chan"),
        P(),
        P("tm", None),
    )
    return jax.shard_map(
        shards, mesh=mesh, in_specs=placed, out_specs=P("chan", "tm", None), check_vma=False
    )
```

```python
import functools

import jax
import jax.numpy as jnp
from jax import lax
from jax.experimental import pallas as pl
from jax.experimental.pallas import tpu as pltpu
from jax.sharding import PartitionSpec as P

C = 512
GROUPS = 32
H = 16
W = 32
CELLS = H * W
GROUP_WIDTH = C // GROUPS
PIECES = 8
TAPS = 27
LANES = 128
VMEM_BYTES = 9 * 1024 * 1024

norm_eps = 1e-06


def clip_start(clip_ref, g):
    first = jnp.int32(0)
    running = jnp.int32(0)
    for c in range(clip_ref.shape[0]):
        first = jnp.where(running <= g, jnp.maximum(first, running), first)
        running = running + clip_ref[c]
    return first


def group_sum(grouped):
    tiles = [grouped[:, :, i : i + LANES] for i in range(0, CELLS, LANES)]
    while len(tiles) > 1:
        tiles = [x + y for x, y in zip(tiles[::2], tiles[1::2])]
    folded = tiles[0][:, :8] + tiles[0][:, 8:]
    return jnp.sum(jnp.sum(folded, axis=1, keepdims=True), axis=2, keepdims=True)


def group_norm(total, gain, bias):
    own = total.shape[0]
    grouped = total.reshape(own // GROUP_WIDTH, GROUP_WIDTH, CELLS)
    scale = 1.0 / (GROUP_WIDTH * CELLS)
    centred = grouped - group_sum(grouped) * scale
    variance = group_sum(centred * centred) * scale
    normed = (centred * lax.rsqrt(variance + norm_eps)).reshape(own, CELLS)
    return normed * gain + bias


def as_column(row):
    count = row.shape[1]
    return jnp.transpose(jnp.broadcast_to(row, (count, count)))[:, :1]


def finished(total, gain, bias, residual):
    normed = group_norm(total, gain, bias)
    activated = normed / (1.0 + jnp.exp(-normed))
    return (activated + residual.astype(jnp.float32)).astype(jnp.bfloat16)


def piece_starts(piece_rows):
    place = lax.axis_index("tm") % PIECES
    return [
        pl.multiple_of(jnp.bitwise_xor(place, i) * piece_rows, piece_rows) for i in range(PIECES)
    ]


def store_in_order(ref, total):
    rows = total.shape[0] // PIECES
    for block, start in enumerate(piece_starts(rows)):
        ref[pl.ds(start, rows), :] = total[block * rows : (block + 1) * rows]


def store_shifted(ref, index, frame):
    shard = frame.shape[0]
    column = lax.broadcasted_iota(jnp.int32, (1, CELLS), 1) % W
    zero = jnp.zeros_like(frame)
    ref[(*index, pl.ds(0, shard))] = jnp.where(column > 0, pltpu.roll(frame, 1, 1), zero)
    ref[(*index, pl.ds(shard, shard))] = frame
    ref[(*index, pl.ds(2 * shard, shard))] = jnp.where(
        column < W - 1, pltpu.roll(frame, CELLS - 1, 1), zero
    )


def row_taps(pieces, inputs, time_taps):
    weights = []
    for a in range(3):
        for block in range(PIECES):
            row = [
                part[block][9 * k + 3 * a + b] for part in pieces for k in time_taps for b in range(3)
            ]
            weights.append(jnp.concatenate(row, axis=1))
    product = jnp.dot(
        jnp.concatenate(weights, axis=0),
        jnp.concatenate(inputs, axis=0),
        preferred_element_type=jnp.float32,
    )
    own = product.shape[0] // 3
    cell = lax.broadcasted_iota(jnp.int32, (1, CELLS), 1)
    up = pltpu.roll(product[:own], W, 1)
    down = pltpu.roll(product[2 * own :], CELLS - W, 1)
    return (
        jnp.where(cell >= W, up, 0.0)
        + product[own : 2 * own]
        + jnp.where(cell < CELLS - W, down, 0.0)
    )


def conv_kernel(parts, slots_of, groups, *refs):
    refs = list(refs)
    clip_ref = refs.pop(0)
    frame_refs = [refs.pop(0) for _ in range(parts)]
    weight_refs = [refs.pop(0) for _ in range(1 if slots_of is None else PIECES)]
    sum_refs = [None if slots_of is None else refs.pop(0) for _ in groups]
    out_refs = [refs.pop(0) for _ in groups]
    shifted_ref = refs.pop(0)
    frame_count, shard, _ = frame_refs[0].shape
    own = out_refs[0].shape[1]
    first_frame = lax.axis_index("tm") * frame_count
    starts = piece_starts(own // PIECES)
    for p in range(parts):
        for f in range(0 if "own" in groups else frame_count // 2, frame_count):
            store_shifted(shifted_ref, (p, f), frame_refs[p][f])
        shifted_ref[p, frame_count] = jnp.zeros_like(shifted_ref[p, frame_count])

    def weight_rows(p, i):
        if slots_of is None:
            return weight_refs[0][:, pl.ds(starts[i], own // PIECES), :]
        return weight_refs[i][slots_of[p]]

    def convolved(j, time_taps):
        g = first_frame + j
        first = clip_start(clip_ref, g)
        inputs = []
        for p in range(parts):
            for k in time_taps:
                source = jnp.maximum(g - 2 + k, first) - first_frame
                source = jnp.where(source < 0, frame_count, jnp.minimum(source, frame_count))
                inputs.append(shifted_ref[p, source])
        pieces = [[weight_rows(p, i) for i in range(PIECES)] for p in range(parts)]
        return row_taps(pieces, inputs, time_taps)

    for group, out_ref, sum_ref in zip(groups, out_refs, sum_refs):
        if group == "next":
            for i, time_taps in enumerate(((0, 1), (0,))):
                total = convolved(frame_count + i, time_taps)
                if sum_ref is not None:
                    total = total + sum_ref[i]
                if groups == ("next",):
                    store_in_order(out_ref.at[i], total)
                else:
                    out_ref[i] = total
            continue

        def one_frame(j, carry, out_ref=out_ref, sum_ref=sum_ref):
            total = convolved(j, (0, 1, 2))
            out_ref[j] = total if sum_ref is None else total + sum_ref[j]
            return carry

        lax.fori_loop(0, frame_count, one_frame, 0)


def conv_parts(clip_lengths, shards_in, weights, slots_of, groups, sums=()):
    frame_count, shard, cells = shards_in[0].shape
    own, parts = shard, len(shards_in)
    vectors = pl.BlockSpec(memory_space=pltpu.VMEM)
    operands = [clip_lengths, *shards_in, *weights, *sums]
    frames = {"own": frame_count, "next": frame_count // 2}
    return pl.pallas_call(
        functools.partial(conv_kernel, parts, slots_of, groups),
        out_shape=[
            jax.ShapeDtypeStruct((frames[group], own, cells), jnp.float32) for group in groups
        ],
        in_specs=[pl.BlockSpec(memory_space=pltpu.SMEM)] + [vectors] * (len(operands) - 1),
        out_specs=[vectors] * len(groups),
        scratch_shapes=[pltpu.VMEM((parts, frame_count + 1, 3 * shard, cells), jnp.bfloat16)],
        compiler_params=pltpu.CompilerParams(vmem_limit_bytes=VMEM_BYTES),
        cost_estimate=pl.CostEstimate(flops=1024, bytes_accessed=1024, transcendentals=0),
        name="conv_parts",
    )(*operands)


def shift_kernel(frames_ref, out_ref):
    for f in range(frames_ref.shape[0]):
        store_shifted(out_ref, (f,), frames_ref[f])


def shifted_frames(frames):
    count, shard, cells = frames.shape
    return pl.pallas_call(
        shift_kernel,
        out_shape=jax.ShapeDtypeStruct((count, 3 * shard, cells), jnp.bfloat16),
        in_specs=[pl.BlockSpec(memory_space=pltpu.VMEM)],
        out_specs=pl.BlockSpec(memory_space=pltpu.VMEM),
        compiler_params=pltpu.CompilerParams(vmem_limit_bytes=VMEM_BYTES),
        cost_estimate=pl.CostEstimate(flops=1500000000, bytes_accessed=1024, transcendentals=0),
        name="shifted_frames",
    )(frames)


def last_kernel(slot, far, *refs):
    refs = list(refs)
    clip_ref, shifted_ref, halo_ref = refs[:3]
    weight_refs = refs[3 : 3 + PIECES]
    sum_ref, arrived_ref, residual_ref, gain_ref, bias_ref = refs[3 + PIECES : 8 + PIECES]
    out_ref, earlier_ref, total_ref = refs[8 + PIECES :]
    frame_count = shifted_ref.shape[0]
    half = frame_count // 2
    slab = lax.axis_index("tm")
    first_frame = slab * frame_count
    tail = (slab % 2 == 1) if far else (slab % 2 == 0)
    gain, bias = as_column(gain_ref[...]), as_column(bias_ref[...])

    @pl.when(jnp.logical_not(tail))
    def _():
        for f in range(half):
            store_shifted(earlier_ref, (f,), halo_ref[f])

    @pl.when(tail)
    def _():
        for f in range(half):
            earlier_ref[f] = jnp.zeros_like(earlier_ref[f])

    def one_frame(i, carry):
        j = jnp.where(tail, i + half, i)
        g = first_frame + j
        first = clip_start(clip_ref, g)
        inputs = []
        for k in range(3):
            source = jnp.maximum(g - 2 + k, first) - first_frame
            inputs.append(
                jnp.where(
                    source < 0,
                    earlier_ref[jnp.clip(source + 2, 0, half - 1)],
                    shifted_ref[jnp.maximum(source, 0)],
                )
            )
        pieces = [[ref[min(slot, ref.shape[0] - 1)] for ref in weight_refs]]
        total = row_taps(pieces, inputs, (0, 1, 2)) + sum_ref[j]
        store_in_order(total_ref, total)
        total = total_ref[...] + jnp.where(tail, 0.0, arrived_ref[i])
        out_ref[i] = finished(total, gain, bias, residual_ref[j])
        return carry

    lax.fori_loop(0, half, one_frame, 0)


def last_part(clip_lengths, far, slot, *operands):
    shifted, halo = operands[:2]
    half, shard, cells = halo.shape
    vectors = pl.BlockSpec(memory_space=pltpu.VMEM)
    return pl.pallas_call(
        functools.partial(last_kernel, slot, far),
        out_shape=jax.ShapeDtypeStruct((half, shard, cells), jnp.bfloat16),
        in_specs=[pl.BlockSpec(memory_space=pltpu.SMEM)] + [vectors] * len(operands),
        out_specs=vectors,
        scratch_shapes=[
            pltpu.VMEM((half, 3 * shard, cells), jnp.bfloat16),
            pltpu.VMEM((shard, cells), jnp.float32),
        ],
        compiler_params=pltpu.CompilerParams(vmem_limit_bytes=VMEM_BYTES),
        cost_estimate=pl.CostEstimate(flops=1024 if far else 1024, bytes_accessed=1024, transcendentals=0),
        name="last_part",
    )(clip_lengths, *operands)


def slot_of(bounds_ref, frame_count, position):
    first = lax.axis_index("tm") * frame_count - frame_count // 2
    return position + first - bounds_ref[0, 0], bounds_ref[0, 1] - bounds_ref[0, 0]


def near_position(place, half):
    odd = lax.axis_index("tm") % 2 == 1
    return jnp.where(odd, place * half, (3 - place) * half)


def window_kernel(bounds_ref, near_ref, far_ref, far_in_ref, out_ref):
    half = near_ref.shape[0]
    capacity = out_ref.shape[0]
    for place, pair in enumerate((near_ref, far_ref, far_in_ref), 1):
        for i in range(half):
            slot, size = slot_of(bounds_ref, 2 * half, near_position(place, half) + i)

            @pl.when((slot >= 0) & (slot < size))
            def _():
                out_ref[slot] = pair[i].astype(jnp.float32)

    for slot in range(capacity):

        @pl.when(slot >= size)
        def _():
            out_ref[slot] = jnp.zeros_like(out_ref[slot])


def slots_kernel(bounds_ref, window_ref, near_in_ref, out_ref):
    capacity, channels, _ = window_ref.shape
    half = near_in_ref.shape[0]
    position = near_position(0, half)
    slot, size = slot_of(bounds_ref, 2 * half, position)
    rows = 16
    for start in range(0, channels, rows):
        frames = [window_ref[w, start : start + rows, :] for w in range(capacity)]
        for i in range(half):
            frame = near_in_ref[i, start : start + rows, :].astype(jnp.float32)
            for w in range(capacity):
                frames[w] = jnp.where((slot + i == w) & (w < size), frame, frames[w])
        block = jnp.stack(frames)
        out_ref[start : start + rows] = jnp.swapaxes(block, 0, 1).astype(jnp.bfloat16)


def slots(bounds, near_in, near, far, far_in):
    half, channels, cells = near.shape
    capacity = 4 * half
    scalars = pl.BlockSpec(memory_space=pltpu.SMEM)
    vectors = pl.BlockSpec(memory_space=pltpu.VMEM)
    window = pl.pallas_call(
        window_kernel,
        out_shape=jax.ShapeDtypeStruct((capacity, channels, cells), jnp.float32),
        in_specs=[scalars] + [vectors] * 3,
        out_specs=vectors,
        compiler_params=pltpu.CompilerParams(vmem_limit_bytes=VMEM_BYTES),
        cost_estimate=pl.CostEstimate(flops=1000000000, bytes_accessed=1024, transcendentals=0),
        name="window",
    )(bounds, near, far, far_in)
    return pl.pallas_call(
        slots_kernel,
        out_shape=jax.ShapeDtypeStruct((channels, capacity, cells), jnp.bfloat16),
        in_specs=[scalars] + [vectors] * 2,
        out_specs=vectors,
        compiler_params=pltpu.CompilerParams(vmem_limit_bytes=VMEM_BYTES),
        name="slots",
    )(bounds, window, near_in)


def xor_permute(array, axis, bits):
    return lax.ppermute(array, axis, [(i, i ^ bits) for i in range(lax.axis_size(axis))])


def weight_blocks(by_tap):
    _, out_channels, shard = by_tap.shape
    chan_count = lax.axis_size("chan")
    own = out_channels // chan_count
    piece_rows = own // PIECES
    piece = lax.axis_index("tm") % PIECES
    me = lax.axis_index("chan")
    pieces = [
        lax.dynamic_slice(
            by_tap,
            (0, jnp.bitwise_xor(me, s) * own + piece * piece_rows, 0),
            (TAPS, piece_rows, shard),
        )
        for s in range(1, chan_count)
    ]
    return lax.dynamic_slice(by_tap, (0, me * own, 0), (TAPS, own, shard)), pieces


def shards(latents, conv_weight, norm_gain, norm_bias, clip_lengths, slab_bounds):
    own, frame_count, cells = latents.shape
    out_channels, _, _, shard = conv_weight.shape
    tm_count = lax.axis_size("tm")

    by_tap = jnp.transpose(conv_weight, (1, 2, 0, 3)).reshape(TAPS, out_channels, shard)
    own_weights, blocks = weight_blocks(by_tap)
    blocks, latents = lax.optimization_barrier((blocks, latents))
    by_frame = jnp.transpose(latents, (1, 0, 2))
    swapped = [xor_permute(block, "chan", s) for s, block in enumerate(blocks, 1)]

    half = frame_count // 2
    swapped[0], by_frame = lax.optimization_barrier((swapped[0], by_frame))
    first = xor_permute(by_frame, "chan", 1)
    swapped, kept = lax.optimization_barrier((jnp.stack(swapped), by_frame))
    second = xor_permute(kept, "chan", 2)
    total, following = conv_parts(clip_lengths, [by_frame], [own_weights], None, ("own", "next"))
    same_core = [swapped] + [xor_permute(swapped, "tm", bits) for bits in range(2, PIECES, 2)]
    same_core, total, first = lax.optimization_barrier((same_core, total, first))
    other_core = [xor_permute(piece, "tm", 1) for piece in same_core]
    weights = [piece for pair in zip(same_core, other_core) for piece in pair]
    third = xor_permute(second, "chan", 1)
    chan_count = lax.axis_size("chan")
    third_halo = lax.ppermute(
        second[half:],
        ("tm", "chan"),
        [
            (t * chan_count + (c ^ 1), (t + 1) * chan_count + c)
            for t in range(tm_count - 1)
            for c in range(chan_count)
        ],
    )
    pair, slots_of = [first, second], (0, 1)
    (following,) = conv_parts(clip_lengths, pair, weights, slots_of, ("next",), [following])
    arrived = lax.ppermute(following, "tm", [(i, i + 1) for i in range(tm_count - 1)])
    (total,) = conv_parts(clip_lengths, pair, weights, slots_of, ("own",), [total])
    operands = [shifted_frames(third), third_halo, *weights, total]
    params = (by_frame, norm_gain.reshape(1, own), norm_bias.reshape(1, own))

    def swapped_pairs(start):
        pairs = range(start, tm_count - 1, 2)
        return [(i, i + 1) for i in pairs] + [(i + 1, i) for i in pairs]

    far = last_part(clip_lengths, True, 2, *operands, arrived, *params)
    far_in = lax.ppermute(far, "tm", swapped_pairs(1))
    arrived, far = lax.optimization_barrier((arrived, far))
    near = last_part(clip_lengths, False, 2, *operands, arrived, *params)
    near_in = lax.ppermute(near, "tm", swapped_pairs(0))
    return slots(slab_bounds, near_in, near, far, far_in)


def solution(mesh):
    placed = (
        P("chan", "tm", None),
        P(None, None, None, "chan"),
        P("chan"),
        P("chan"),
        P(),
        P("tm", None),
    )
    return jax.shard_map(
        shards, mesh=mesh, in_specs=placed, out_specs=P("chan", "tm", None), check_vma=False
    )
```

```python
import functools

import jax
import jax.numpy as jnp
from jax import lax
from jax.experimental import pallas as pl
from jax.experimental.pallas import tpu as pltpu
from jax.sharding import PartitionSpec as P

C = 512
GROUPS = 32
H = 16
W = 32
CELLS = H * W
GROUP_WIDTH = C // GROUPS
PIECES = 8
TAPS = 27
LANES = 128
VMEM_BYTES = 9 * 1024 * 1024

norm_eps = 1e-06


def clip_start(clip_ref, g):
    first = jnp.int32(0)
    running = jnp.int32(0)
    for c in range(clip_ref.shape[0]):
        first = jnp.where(running <= g, jnp.maximum(first, running), first)
        running = running + clip_ref[c]
    return first


def group_sum(grouped):
    tiles = [grouped[:, :, i : i + LANES] for i in range(0, CELLS, LANES)]
    while len(tiles) > 1:
        tiles = [x + y for x, y in zip(tiles[::2], tiles[1::2])]
    folded = tiles[0][:, :8] + tiles[0][:, 8:]
    return jnp.sum(jnp.sum(folded, axis=1, keepdims=True), axis=2, keepdims=True)


def group_norm(total, gain, bias):
    own = total.shape[0]
    grouped = total.reshape(own // GROUP_WIDTH, GROUP_WIDTH, CELLS)
    scale = 1.0 / (GROUP_WIDTH * CELLS)
    centred = grouped - group_sum(grouped) * scale
    variance = group_sum(centred * centred) * scale
    normed = (centred * lax.rsqrt(variance + norm_eps)).reshape(own, CELLS)
    return normed * gain + bias


def as_column(row):
    count = row.shape[1]
    return jnp.transpose(jnp.broadcast_to(row, (count, count)))[:, :1]


def finished(total, gain, bias, residual):
    normed = group_norm(total, gain, bias)
    activated = normed / (1.0 + jnp.exp(-normed))
    return (activated + residual.astype(jnp.float32)).astype(jnp.bfloat16)


def piece_starts(piece_rows):
    place = lax.axis_index("tm") % PIECES
    return [
        pl.multiple_of(jnp.bitwise_xor(place, i) * piece_rows, piece_rows) for i in range(PIECES)
    ]


def store_in_order(ref, total):
    rows = total.shape[0] // PIECES
    for block, start in enumerate(piece_starts(rows)):
        ref[pl.ds(start, rows), :] = total[block * rows : (block + 1) * rows]


def store_shifted(ref, index, frame):
    shard = frame.shape[0]
    column = lax.broadcasted_iota(jnp.int32, (1, CELLS), 1) % W
    zero = jnp.zeros_like(frame)
    ref[(*index, pl.ds(0, shard))] = jnp.where(column > 0, pltpu.roll(frame, 1, 1), zero)
    ref[(*index, pl.ds(shard, shard))] = frame
    ref[(*index, pl.ds(2 * shard, shard))] = jnp.where(
        column < W - 1, pltpu.roll(frame, CELLS - 1, 1), zero
    )


def row_taps(pieces, inputs, time_taps):
    weights = []
    for a in range(3):
        for block in range(PIECES):
            row = [
                part[block][9 * k + 3 * a + b] for part in pieces for k in time_taps for b in range(3)
            ]
            weights.append(jnp.concatenate(row, axis=1))
    product = jnp.dot(
        jnp.concatenate(weights, axis=0),
        jnp.concatenate(inputs, axis=0),
        preferred_element_type=jnp.float32,
    )
    own = product.shape[0] // 3
    cell = lax.broadcasted_iota(jnp.int32, (1, CELLS), 1)
    up = pltpu.roll(product[:own], W, 1)
    down = pltpu.roll(product[2 * own :], CELLS - W, 1)
    return (
        jnp.where(cell >= W, up, 0.0)
        + product[own : 2 * own]
        + jnp.where(cell < CELLS - W, down, 0.0)
    )


def conv_kernel(parts, slots_of, groups, *refs):
    refs = list(refs)
    clip_ref = refs.pop(0)
    frame_refs = [refs.pop(0) for _ in range(parts)]
    weight_refs = [refs.pop(0) for _ in range(1 if slots_of is None else PIECES)]
    sum_refs = [None if slots_of is None else refs.pop(0) for _ in groups]
    out_refs = [refs.pop(0) for _ in groups]
    shifted_ref = refs.pop(0)
    frame_count, shard, _ = frame_refs[0].shape
    own = out_refs[0].shape[1]
    first_frame = lax.axis_index("tm") * frame_count
    starts = piece_starts(own // PIECES)
    for p in range(parts):
        for f in range(0 if "own" in groups else frame_count // 2, frame_count):
            store_shifted(shifted_ref, (p, f), frame_refs[p][f])
        shifted_ref[p, frame_count] = jnp.zeros_like(shifted_ref[p, frame_count])

    def weight_rows(p, i):
        if slots_of is None:
            return weight_refs[0][:, pl.ds(starts[i], own // PIECES), :]
        return weight_refs[i][slots_of[p]]

    def convolved(j, time_taps):
        g = first_frame + j
        first = clip_start(clip_ref, g)
        inputs = []
        for p in range(parts):
            for k in time_taps:
                source = jnp.maximum(g - 2 + k, first) - first_frame
                source = jnp.where(source < 0, frame_count, jnp.minimum(source, frame_count))
                inputs.append(shifted_ref[p, source])
        pieces = [[weight_rows(p, i) for i in range(PIECES)] for p in range(parts)]
        return row_taps(pieces, inputs, time_taps)

    for group, out_ref, sum_ref in zip(groups, out_refs, sum_refs):
        if group == "next":
            for i, time_taps in enumerate(((0, 1), (0,))):
                total = convolved(frame_count + i, time_taps)
                if sum_ref is not None:
                    total = total + sum_ref[i]
                if groups == ("next",):
                    store_in_order(out_ref.at[i], total)
                else:
                    out_ref[i] = total
            continue

        for j in range(frame_count):
            total = convolved(j, (0, 1, 2))
            out_ref[j] = total if sum_ref is None else total + sum_ref[j]


def conv_parts(clip_lengths, shards_in, weights, slots_of, groups, sums=()):
    frame_count, shard, cells = shards_in[0].shape
    own, parts = shard, len(shards_in)
    vectors = pl.BlockSpec(memory_space=pltpu.VMEM)
    operands = [clip_lengths, *shards_in, *weights, *sums]
    frames = {"own": frame_count, "next": frame_count // 2}
    return pl.pallas_call(
        functools.partial(conv_kernel, parts, slots_of, groups),
        out_shape=[
            jax.ShapeDtypeStruct((frames[group], own, cells), jnp.float32) for group in groups
        ],
        in_specs=[pl.BlockSpec(memory_space=pltpu.SMEM)] + [vectors] * (len(operands) - 1),
        out_specs=[vectors] * len(groups),
        scratch_shapes=[pltpu.VMEM((parts, frame_count + 1, 3 * shard, cells), jnp.bfloat16)],
        compiler_params=pltpu.CompilerParams(vmem_limit_bytes=VMEM_BYTES),
        cost_estimate=pl.CostEstimate(flops=1024, bytes_accessed=1024, transcendentals=0),
        name="conv_parts",
    )(*operands)


def shift_kernel(frames_ref, halo_ref, out_ref):
    count = frames_ref.shape[0]
    for f in range(count):
        store_shifted(out_ref, (f,), frames_ref[f])
    for f in range(halo_ref.shape[0]):
        store_shifted(out_ref, (count + f,), halo_ref[f])


def shifted_frames(frames, halo):
    count, shard, cells = frames.shape
    return pl.pallas_call(
        shift_kernel,
        out_shape=jax.ShapeDtypeStruct((count + halo.shape[0], 3 * shard, cells), jnp.bfloat16),
        in_specs=[pl.BlockSpec(memory_space=pltpu.VMEM)] * 2,
        out_specs=pl.BlockSpec(memory_space=pltpu.VMEM),
        compiler_params=pltpu.CompilerParams(vmem_limit_bytes=VMEM_BYTES),
        cost_estimate=pl.CostEstimate(flops=1500000000, bytes_accessed=1024, transcendentals=0),
        name="shifted_frames",
    )(frames, halo)


def last_kernel(slot, far, *refs):
    refs = list(refs)
    clip_ref, shifted_ref = refs[:2]
    weight_refs = refs[2 : 2 + PIECES]
    sum_ref, arrived_ref, residual_ref, gain_ref, bias_ref = refs[2 + PIECES : 7 + PIECES]
    out_ref, total_ref = refs[7 + PIECES :]
    frame_count, half = residual_ref.shape[0], arrived_ref.shape[0]
    slab = lax.axis_index("tm")
    first_frame = slab * frame_count
    tail = (slab % 2 == 1) if far else (slab % 2 == 0)
    gain, bias = as_column(gain_ref[...]), as_column(bias_ref[...])

    for i in range(half):
        j = jnp.where(tail, i + half, i)
        g = first_frame + j
        first = clip_start(clip_ref, g)
        inputs = []
        for k in range(3):
            source = jnp.maximum(g - 2 + k, first) - first_frame
            inputs.append(shifted_ref[jnp.where(source < 0, source + frame_count + half, source)])
        pieces = [[ref[min(slot, ref.shape[0] - 1)] for ref in weight_refs]]
        total = row_taps(pieces, inputs, (0, 1, 2)) + sum_ref[j]
        store_in_order(total_ref.at[i], total)
        total = total_ref[i] + jnp.where(tail, 0.0, arrived_ref[i])
        out_ref[i] = finished(total, gain, bias, residual_ref[j])


def last_part(clip_lengths, far, slot, *operands):
    half, shard, cells = operands[2 + PIECES].shape
    vectors = pl.BlockSpec(memory_space=pltpu.VMEM)
    return pl.pallas_call(
        functools.partial(last_kernel, slot, far),
        out_shape=jax.ShapeDtypeStruct((half, shard, cells), jnp.bfloat16),
        in_specs=[pl.BlockSpec(memory_space=pltpu.SMEM)] + [vectors] * len(operands),
        out_specs=vectors,
        scratch_shapes=[
            pltpu.VMEM((half, shard, cells), jnp.float32),
        ],
        compiler_params=pltpu.CompilerParams(vmem_limit_bytes=VMEM_BYTES),
        cost_estimate=pl.CostEstimate(flops=1024 if far else 1024, bytes_accessed=1024, transcendentals=0),
        name="last_part",
    )(clip_lengths, *operands)


def slot_of(bounds_ref, frame_count, position):
    first = lax.axis_index("tm") * frame_count - frame_count // 2
    return position + first - bounds_ref[0, 0], bounds_ref[0, 1] - bounds_ref[0, 0]


def near_position(place, half):
    odd = lax.axis_index("tm") % 2 == 1
    return jnp.where(odd, place * half, (3 - place) * half)


def window_kernel(bounds_ref, near_ref, far_ref, far_in_ref, out_ref):
    half = near_ref.shape[0]
    capacity = out_ref.shape[0]
    for place, pair in enumerate((near_ref, far_ref, far_in_ref), 1):
        for i in range(half):
            slot, size = slot_of(bounds_ref, 2 * half, near_position(place, half) + i)

            @pl.when((slot >= 0) & (slot < size))
            def _():
                out_ref[slot] = pair[i].astype(jnp.float32)

    for slot in range(capacity):

        @pl.when(slot >= size)
        def _():
            out_ref[slot] = jnp.zeros_like(out_ref[slot])


def slots_kernel(bounds_ref, window_ref, near_in_ref, out_ref):
    capacity, channels, _ = window_ref.shape
    half = near_in_ref.shape[0]
    position = near_position(0, half)
    slot, size = slot_of(bounds_ref, 2 * half, position)
    rows = 16
    for start in range(0, channels, rows):
        frames = [window_ref[w, start : start + rows, :] for w in range(capacity)]
        for i in range(half):
            frame = near_in_ref[i, start : start + rows, :].astype(jnp.float32)
            for w in range(capacity):
                frames[w] = jnp.where((slot + i == w) & (w < size), frame, frames[w])
        block = jnp.stack(frames)
        out_ref[start : start + rows] = jnp.swapaxes(block, 0, 1).astype(jnp.bfloat16)


def slots(bounds, near_in, near, far, far_in):
    half, channels, cells = near.shape
    capacity = 4 * half
    scalars = pl.BlockSpec(memory_space=pltpu.SMEM)
    vectors = pl.BlockSpec(memory_space=pltpu.VMEM)
    window = pl.pallas_call(
        window_kernel,
        out_shape=jax.ShapeDtypeStruct((capacity, channels, cells), jnp.float32),
        in_specs=[scalars] + [vectors] * 3,
        out_specs=vectors,
        compiler_params=pltpu.CompilerParams(vmem_limit_bytes=VMEM_BYTES),
        cost_estimate=pl.CostEstimate(flops=1000000000, bytes_accessed=1024, transcendentals=0),
        name="window",
    )(bounds, near, far, far_in)
    return pl.pallas_call(
        slots_kernel,
        out_shape=jax.ShapeDtypeStruct((channels, capacity, cells), jnp.bfloat16),
        in_specs=[scalars] + [vectors] * 2,
        out_specs=vectors,
        compiler_params=pltpu.CompilerParams(vmem_limit_bytes=VMEM_BYTES),
        name="slots",
    )(bounds, window, near_in)


def xor_permute(array, axis, bits):
    return lax.ppermute(array, axis, [(i, i ^ bits) for i in range(lax.axis_size(axis))])


def weight_blocks(by_tap):
    _, out_channels, shard = by_tap.shape
    chan_count = lax.axis_size("chan")
    own = out_channels // chan_count
    piece_rows = own // PIECES
    piece = lax.axis_index("tm") % PIECES
    me = lax.axis_index("chan")
    pieces = [
        lax.dynamic_slice(
            by_tap,
            (0, jnp.bitwise_xor(me, s) * own + piece * piece_rows, 0),
            (TAPS, piece_rows, shard),
        )
        for s in range(1, chan_count)
    ]
    return lax.dynamic_slice(by_tap, (0, me * own, 0), (TAPS, own, shard)), pieces


def shards(latents, conv_weight, norm_gain, norm_bias, clip_lengths, slab_bounds):
    own, frame_count, cells = latents.shape
    out_channels, _, _, shard = conv_weight.shape
    tm_count = lax.axis_size("tm")

    by_tap = jnp.transpose(conv_weight, (1, 2, 0, 3)).reshape(TAPS, out_channels, shard)
    own_weights, blocks = weight_blocks(by_tap)
    blocks, latents = lax.optimization_barrier((blocks, latents))
    by_frame = jnp.transpose(latents, (1, 0, 2))
    swapped = [xor_permute(block, "chan", s) for s, block in enumerate(blocks, 1)]

    half = frame_count // 2
    swapped[0], by_frame = lax.optimization_barrier((swapped[0], by_frame))
    first = xor_permute(by_frame, "chan", 1)
    swapped, kept = lax.optimization_barrier((jnp.stack(swapped), by_frame))
    second = xor_permute(kept, "chan", 2)
    total, following = conv_parts(clip_lengths, [by_frame], [own_weights], None, ("own", "next"))
    same_core = [swapped] + [xor_permute(swapped, "tm", bits) for bits in range(2, PIECES, 2)]
    same_core, total, first = lax.optimization_barrier((same_core, total, first))
    other_core = [xor_permute(piece, "tm", 1) for piece in same_core]
    weights = [piece for pair in zip(same_core, other_core) for piece in pair]
    third = xor_permute(second, "chan", 1)
    chan_count = lax.axis_size("chan")
    third_halo = lax.ppermute(
        second[half:],
        ("tm", "chan"),
        [
            (t * chan_count + (c ^ 1), (t + 1) * chan_count + c)
            for t in range(tm_count - 1)
            for c in range(chan_count)
        ],
    )
    pair, slots_of = [first, second], (0, 1)
    (following,) = conv_parts(clip_lengths, pair, weights, slots_of, ("next",), [following])
    arrived = lax.ppermute(following, "tm", [(i, i + 1) for i in range(tm_count - 1)])
    (total,) = conv_parts(clip_lengths, pair, weights, slots_of, ("own",), [total])
    operands = [shifted_frames(third, third_halo), *weights, total]
    params = (by_frame, norm_gain.reshape(1, own), norm_bias.reshape(1, own))

    def swapped_pairs(start):
        pairs = range(start, tm_count - 1, 2)
        return [(i, i + 1) for i in pairs] + [(i + 1, i) for i in pairs]

    far = last_part(clip_lengths, True, 2, *operands, arrived, *params)
    far_in = lax.ppermute(far, "tm", swapped_pairs(1))
    arrived, far = lax.optimization_barrier((arrived, far))
    near = last_part(clip_lengths, False, 2, *operands, arrived, *params)
    near_in = lax.ppermute(near, "tm", swapped_pairs(0))
    return slots(slab_bounds, near_in, near, far, far_in)


def solution(mesh):
    placed = (
        P("chan", "tm", None),
        P(None, None, None, "chan"),
        P("chan"),
        P("chan"),
        P(),
        P("tm", None),
    )
    return jax.shard_map(
        shards, mesh=mesh, in_specs=placed, out_specs=P("chan", "tm", None), check_vma=False
    )
```

```python
import functools

import jax
import jax.numpy as jnp
from jax import lax
from jax.experimental import pallas as pl
from jax.experimental.pallas import tpu as pltpu
from jax.sharding import PartitionSpec as P

C = 512
GROUPS = 32
H = 16
W = 32
CELLS = H * W
GROUP_WIDTH = C // GROUPS
PIECES = 8
TAPS = 27
LANES = 128
VMEM_BYTES = 9 * 1024 * 1024

norm_eps = 1e-06


def clip_start(clip_ref, g):
    first = jnp.int32(0)
    running = jnp.int32(0)
    for c in range(clip_ref.shape[0]):
        first = jnp.where(running <= g, jnp.maximum(first, running), first)
        running = running + clip_ref[c]
    return first


def group_sum(grouped):
    tiles = [grouped[:, :, i : i + LANES] for i in range(0, CELLS, LANES)]
    while len(tiles) > 1:
        tiles = [x + y for x, y in zip(tiles[::2], tiles[1::2])]
    folded = tiles[0][:, :8] + tiles[0][:, 8:]
    return jnp.sum(jnp.sum(folded, axis=1, keepdims=True), axis=2, keepdims=True)


def group_norm(total, gain, bias):
    own = total.shape[0]
    grouped = total.reshape(own // GROUP_WIDTH, GROUP_WIDTH, CELLS)
    scale = 1.0 / (GROUP_WIDTH * CELLS)
    centred = grouped - group_sum(grouped) * scale
    variance = group_sum(centred * centred) * scale
    normed = (centred * lax.rsqrt(variance + norm_eps)).reshape(own, CELLS)
    return normed * gain + bias


def as_column(row):
    count = row.shape[1]
    return jnp.transpose(jnp.broadcast_to(row, (count, count)))[:, :1]


def finished(total, gain, bias, residual):
    normed = group_norm(total, gain, bias)
    activated = normed / (1.0 + jnp.exp(-normed))
    return (activated + residual.astype(jnp.float32)).astype(jnp.bfloat16)


def piece_starts(piece_rows):
    place = lax.axis_index("tm") % PIECES
    return [
        pl.multiple_of(jnp.bitwise_xor(place, i) * piece_rows, piece_rows) for i in range(PIECES)
    ]


def store_in_order(ref, total):
    rows = total.shape[0] // PIECES
    for block, start in enumerate(piece_starts(rows)):
        ref[pl.ds(start, rows), :] = total[block * rows : (block + 1) * rows]


def store_shifted(ref, index, frame):
    shard = frame.shape[0]
    column = lax.broadcasted_iota(jnp.int32, (1, CELLS), 1) % W
    zero = jnp.zeros_like(frame)
    ref[(*index, pl.ds(0, shard))] = jnp.where(column > 0, pltpu.roll(frame, 1, 1), zero)
    ref[(*index, pl.ds(shard, shard))] = frame
    ref[(*index, pl.ds(2 * shard, shard))] = jnp.where(
        column < W - 1, pltpu.roll(frame, CELLS - 1, 1), zero
    )


def row_taps(pieces, inputs, time_taps):
    weights = []
    for a in range(3):
        for block in range(PIECES):
            row = [
                part[block][9 * k + 3 * a + b] for part in pieces for k in time_taps for b in range(3)
            ]
            weights.append(jnp.concatenate(row, axis=1))
    product = jnp.dot(
        jnp.concatenate(weights, axis=0),
        jnp.concatenate(inputs, axis=0),
        preferred_element_type=jnp.float32,
    )
    own = product.shape[0] // 3
    cell = lax.broadcasted_iota(jnp.int32, (1, CELLS), 1)
    up = pltpu.roll(product[:own], W, 1)
    down = pltpu.roll(product[2 * own :], CELLS - W, 1)
    return (
        jnp.where(cell >= W, up, 0.0)
        + product[own : 2 * own]
        + jnp.where(cell < CELLS - W, down, 0.0)
    )


def conv_kernel(parts, slots_of, groups, *refs):
    refs = list(refs)
    clip_ref = refs.pop(0)
    frame_refs = [refs.pop(0) for _ in range(parts)]
    weight_refs = [refs.pop(0) for _ in range(1 if slots_of is None else PIECES)]
    sum_refs = [None if slots_of is None else refs.pop(0) for _ in groups]
    out_refs = [refs.pop(0) for _ in groups]
    shifted_ref = refs.pop(0)
    frame_count, shard, _ = frame_refs[0].shape
    own = out_refs[0].shape[1]
    first_frame = lax.axis_index("tm") * frame_count
    starts = piece_starts(own // PIECES)
    for p in range(parts):
        for f in range(0 if "own" in groups else frame_count // 2, frame_count):
            store_shifted(shifted_ref, (p, f), frame_refs[p][f])
        shifted_ref[p, frame_count] = jnp.zeros_like(shifted_ref[p, frame_count])

    def weight_rows(p, i):
        if slots_of is None:
            return weight_refs[0][:, pl.ds(starts[i], own // PIECES), :]
        return weight_refs[i][slots_of[p]]

    def convolved(j, time_taps):
        g = first_frame + j
        first = clip_start(clip_ref, g)
        inputs = []
        for p in range(parts):
            for k in time_taps:
                source = jnp.maximum(g - 2 + k, first) - first_frame
                source = jnp.where(source < 0, frame_count, jnp.minimum(source, frame_count))
                inputs.append(shifted_ref[p, source])
        pieces = [[weight_rows(p, i) for i in range(PIECES)] for p in range(parts)]
        return row_taps(pieces, inputs, time_taps)

    for group, out_ref, sum_ref in zip(groups, out_refs, sum_refs):
        if group == "next":
            for i, time_taps in enumerate(((0, 1), (0,))):
                total = convolved(frame_count + i, time_taps)
                if sum_ref is not None:
                    total = total + sum_ref[i]
                if groups == ("next",):
                    store_in_order(out_ref.at[i], total)
                else:
                    out_ref[i] = total
            continue

        for j in range(frame_count):
            total = convolved(j, (0, 1, 2))
            out_ref[j] = total if sum_ref is None else total + sum_ref[j]


def conv_parts(clip_lengths, shards_in, weights, slots_of, groups, sums=()):
    frame_count, shard, cells = shards_in[0].shape
    own, parts = shard, len(shards_in)
    vectors = pl.BlockSpec(memory_space=pltpu.VMEM)
    operands = [clip_lengths, *shards_in, *weights, *sums]
    frames = {"own": frame_count, "next": frame_count // 2}
    return pl.pallas_call(
        functools.partial(conv_kernel, parts, slots_of, groups),
        out_shape=[
            jax.ShapeDtypeStruct((frames[group], own, cells), jnp.float32) for group in groups
        ],
        in_specs=[pl.BlockSpec(memory_space=pltpu.SMEM)] + [vectors] * (len(operands) - 1),
        out_specs=[vectors] * len(groups),
        scratch_shapes=[pltpu.VMEM((parts, frame_count + 1, 3 * shard, cells), jnp.bfloat16)],
        compiler_params=pltpu.CompilerParams(vmem_limit_bytes=VMEM_BYTES),
        cost_estimate=pl.CostEstimate(flops=1024, bytes_accessed=1024, transcendentals=0),
        name="conv_parts",
    )(*operands)


def shift_kernel(*refs):
    *pair_refs, out_ref = refs
    half = pair_refs[0].shape[0]
    for i, pair_ref in enumerate(pair_refs):
        for f in range(half):
            store_shifted(out_ref, (i * half + f,), pair_ref[f])


def shifted_frames(*pairs):
    half, shard, cells = pairs[0].shape
    return pl.pallas_call(
        shift_kernel,
        out_shape=jax.ShapeDtypeStruct((len(pairs) * half, 3 * shard, cells), jnp.bfloat16),
        in_specs=[pl.BlockSpec(memory_space=pltpu.VMEM)] * len(pairs),
        out_specs=pl.BlockSpec(memory_space=pltpu.VMEM),
        compiler_params=pltpu.CompilerParams(vmem_limit_bytes=VMEM_BYTES),
        cost_estimate=pl.CostEstimate(flops=1500000000, bytes_accessed=1024, transcendentals=0),
        name="shifted_frames",
    )(*pairs)


def last_kernel(slot, far, *refs):
    refs = list(refs)
    clip_ref, shifted_ref = refs[:2]
    weight_refs = refs[2 : 2 + PIECES]
    sum_ref, arrived_ref, residual_ref, gain_ref, bias_ref = refs[2 + PIECES : 7 + PIECES]
    out_ref, total_ref = refs[7 + PIECES :]
    frame_count, half = residual_ref.shape[0], arrived_ref.shape[0]
    slab = lax.axis_index("tm")
    first_frame = slab * frame_count
    tail = (slab % 2 == 1) if far else (slab % 2 == 0)
    gain, bias = as_column(gain_ref[...]), as_column(bias_ref[...])

    for i in range(half):
        j = jnp.where(tail, i + half, i)
        g = first_frame + j
        first = clip_start(clip_ref, g)
        inputs = []
        for k in range(3):
            source = jnp.maximum(g - 2 + k, first) - first_frame
            inputs.append(shifted_ref[jnp.where(source < 0, source + frame_count + half, source)])
        pieces = [[ref[min(slot, ref.shape[0] - 1)] for ref in weight_refs]]
        total = row_taps(pieces, inputs, (0, 1, 2)) + sum_ref[j]
        store_in_order(total_ref.at[i], total)
        total = total_ref[i] + jnp.where(tail, 0.0, arrived_ref[i])
        out_ref[i] = finished(total, gain, bias, residual_ref[j])


def last_part(clip_lengths, far, slot, *operands):
    half, shard, cells = operands[2 + PIECES].shape
    vectors = pl.BlockSpec(memory_space=pltpu.VMEM)
    return pl.pallas_call(
        functools.partial(last_kernel, slot, far),
        out_shape=jax.ShapeDtypeStruct((half, shard, cells), jnp.bfloat16),
        in_specs=[pl.BlockSpec(memory_space=pltpu.SMEM)] + [vectors] * len(operands),
        out_specs=vectors,
        scratch_shapes=[
            pltpu.VMEM((half, shard, cells), jnp.float32),
        ],
        compiler_params=pltpu.CompilerParams(vmem_limit_bytes=VMEM_BYTES),
        cost_estimate=pl.CostEstimate(flops=1024 if far else 1024, bytes_accessed=1024, transcendentals=0),
        name="last_part",
    )(clip_lengths, *operands)


def slot_of(bounds_ref, frame_count, position):
    first = lax.axis_index("tm") * frame_count - frame_count // 2
    return position + first - bounds_ref[0, 0], bounds_ref[0, 1] - bounds_ref[0, 0]


def near_position(place, half):
    odd = lax.axis_index("tm") % 2 == 1
    return jnp.where(odd, place * half, (3 - place) * half)


def window_kernel(bounds_ref, near_ref, far_ref, far_in_ref, out_ref):
    half = near_ref.shape[0]
    capacity = out_ref.shape[0]
    for place, pair in enumerate((near_ref, far_ref, far_in_ref), 1):
        for i in range(half):
            slot, size = slot_of(bounds_ref, 2 * half, near_position(place, half) + i)

            @pl.when((slot >= 0) & (slot < size))
            def _():
                out_ref[slot] = pair[i].astype(jnp.float32)

    for slot in range(capacity):

        @pl.when(slot >= size)
        def _():
            out_ref[slot] = jnp.zeros_like(out_ref[slot])


def slots_kernel(bounds_ref, window_ref, near_in_ref, out_ref):
    capacity, channels, _ = window_ref.shape
    half = near_in_ref.shape[0]
    position = near_position(0, half)
    slot, size = slot_of(bounds_ref, 2 * half, position)
    rows = 16
    for start in range(0, channels, rows):
        frames = [window_ref[w, start : start + rows, :] for w in range(capacity)]
        for i in range(half):
            frame = near_in_ref[i, start : start + rows, :].astype(jnp.float32)
            for w in range(capacity):
                frames[w] = jnp.where((slot + i == w) & (w < size), frame, frames[w])
        block = jnp.stack(frames)
        out_ref[start : start + rows] = jnp.swapaxes(block, 0, 1).astype(jnp.bfloat16)


def slots(bounds, near_in, near, far, far_in):
    half, channels, cells = near.shape
    capacity = 4 * half
    scalars = pl.BlockSpec(memory_space=pltpu.SMEM)
    vectors = pl.BlockSpec(memory_space=pltpu.VMEM)
    window = pl.pallas_call(
        window_kernel,
        out_shape=jax.ShapeDtypeStruct((capacity, channels, cells), jnp.float32),
        in_specs=[scalars] + [vectors] * 3,
        out_specs=vectors,
        compiler_params=pltpu.CompilerParams(vmem_limit_bytes=VMEM_BYTES),
        cost_estimate=pl.CostEstimate(flops=1000000000, bytes_accessed=1024, transcendentals=0),
        name="window",
    )(bounds, near, far, far_in)
    return pl.pallas_call(
        slots_kernel,
        out_shape=jax.ShapeDtypeStruct((channels, capacity, cells), jnp.bfloat16),
        in_specs=[scalars] + [vectors] * 2,
        out_specs=vectors,
        compiler_params=pltpu.CompilerParams(vmem_limit_bytes=VMEM_BYTES),
        name="slots",
    )(bounds, window, near_in)


def xor_permute(array, axis, bits):
    return lax.ppermute(array, axis, [(i, i ^ bits) for i in range(lax.axis_size(axis))])


def weight_blocks(by_tap):
    _, out_channels, shard = by_tap.shape
    chan_count = lax.axis_size("chan")
    own = out_channels // chan_count
    piece_rows = own // PIECES
    piece = lax.axis_index("tm") % PIECES
    me = lax.axis_index("chan")
    pieces = [
        lax.dynamic_slice(
            by_tap,
            (0, jnp.bitwise_xor(me, s) * own + piece * piece_rows, 0),
            (TAPS, piece_rows, shard),
        )
        for s in range(1, chan_count)
    ]
    return lax.dynamic_slice(by_tap, (0, me * own, 0), (TAPS, own, shard)), pieces


def shards(latents, conv_weight, norm_gain, norm_bias, clip_lengths, slab_bounds):
    own, frame_count, cells = latents.shape
    out_channels, _, _, shard = conv_weight.shape
    tm_count = lax.axis_size("tm")

    by_tap = jnp.transpose(conv_weight, (1, 2, 0, 3)).reshape(TAPS, out_channels, shard)
    own_weights, blocks = weight_blocks(by_tap)
    blocks, latents = lax.optimization_barrier((blocks, latents))
    by_frame = jnp.transpose(latents, (1, 0, 2))
    swapped = [xor_permute(block, "chan", s) for s, block in enumerate(blocks, 1)]

    half = frame_count // 2
    swapped[0], by_frame = lax.optimization_barrier((swapped[0], by_frame))
    first = xor_permute(by_frame, "chan", 1)
    swapped, kept = lax.optimization_barrier((jnp.stack(swapped), by_frame))
    second = xor_permute(kept, "chan", 2)
    total, following = conv_parts(clip_lengths, [by_frame], [own_weights], None, ("own", "next"))
    same_core = [swapped] + [xor_permute(swapped, "tm", bits) for bits in range(2, PIECES, 2)]
    same_core, total, first = lax.optimization_barrier((same_core, total, first))
    other_core = [xor_permute(piece, "tm", 1) for piece in same_core]
    weights = [piece for pair in zip(same_core, other_core) for piece in pair]
    third_tail = xor_permute(second[half:], "chan", 1)
    third_tail, second_head = lax.optimization_barrier((third_tail, second[:half]))
    third_head = xor_permute(second_head, "chan", 1)
    pair, slots_of = [first, second], (0, 1)
    (following,) = conv_parts(clip_lengths, pair, weights, slots_of, ("next",), [following])
    arrived = lax.ppermute(following, "tm", [(i, i + 1) for i in range(tm_count - 1)])
    halo = lax.ppermute(third_tail, "tm", [(i, i + 1) for i in range(tm_count - 1)])
    (total,) = conv_parts(clip_lengths, pair, weights, slots_of, ("own",), [total])
    operands = [shifted_frames(third_head, third_tail, halo), *weights, total]
    params = (by_frame, norm_gain.reshape(1, own), norm_bias.reshape(1, own))

    def swapped_pairs(start):
        pairs = range(start, tm_count - 1, 2)
        return [(i, i + 1) for i in pairs] + [(i + 1, i) for i in pairs]

    far = last_part(clip_lengths, True, 2, *operands, arrived, *params)
    far_in = lax.ppermute(far, "tm", swapped_pairs(1))
    arrived, far = lax.optimization_barrier((arrived, far))
    near = last_part(clip_lengths, False, 2, *operands, arrived, *params)
    near_in = lax.ppermute(near, "tm", swapped_pairs(0))
    return slots(slab_bounds, near_in, near, far, far_in)


def solution(mesh):
    placed = (
        P("chan", "tm", None),
        P(None, None, None, "chan"),
        P("chan"),
        P("chan"),
        P(),
        P("tm", None),
    )
    return jax.shard_map(
        shards, mesh=mesh, in_specs=placed, out_specs=P("chan", "tm", None), check_vma=False
    )
```

```python
import functools

import jax
import jax.numpy as jnp
from jax import lax
from jax.experimental import pallas as pl
from jax.experimental.pallas import tpu as pltpu
from jax.sharding import PartitionSpec as P

C = 512
GROUPS = 32
H = 16
W = 32
CELLS = H * W
GROUP_WIDTH = C // GROUPS
PIECES = 8
TAPS = 27
LANES = 128
STAGE = 32
VMEM_BYTES = 9 * 1024 * 1024

norm_eps = 1e-06


def clip_start(clip_ref, g):
    first = jnp.int32(0)
    running = jnp.int32(0)
    for c in range(clip_ref.shape[0]):
        first = jnp.where(running <= g, jnp.maximum(first, running), first)
        running = running + clip_ref[c]
    return first


def group_sum(grouped):
    tiles = [grouped[:, :, i : i + LANES] for i in range(0, CELLS, LANES)]
    while len(tiles) > 1:
        tiles = [x + y for x, y in zip(tiles[::2], tiles[1::2])]
    folded = tiles[0][:, :8] + tiles[0][:, 8:]
    return jnp.sum(jnp.sum(folded, axis=1, keepdims=True), axis=2, keepdims=True)


def group_norm(total, gain, bias):
    own = total.shape[0]
    grouped = total.reshape(own // GROUP_WIDTH, GROUP_WIDTH, CELLS)
    scale = 1.0 / (GROUP_WIDTH * CELLS)
    centred = grouped - group_sum(grouped) * scale
    variance = group_sum(centred * centred) * scale
    normed = (centred * lax.rsqrt(variance + norm_eps)).reshape(own, CELLS)
    return normed * gain + bias


def as_column(row):
    count = row.shape[1]
    return jnp.transpose(jnp.broadcast_to(row, (count, count)))[:, :1]


def finished(total, gain, bias, residual):
    normed = group_norm(total, gain, bias)
    activated = normed / (1.0 + jnp.exp(-normed))
    return (activated + residual.astype(jnp.float32)).astype(jnp.bfloat16)


def piece_starts(piece_rows):
    place = lax.axis_index("tm") % PIECES
    return [
        pl.multiple_of(jnp.bitwise_xor(place, i) * piece_rows, piece_rows) for i in range(PIECES)
    ]


def store_in_order(ref, total):
    rows = total.shape[0] // PIECES
    for block, start in enumerate(piece_starts(rows)):
        ref[pl.ds(start, rows), :] = total[block * rows : (block + 1) * rows]


def store_shifted(ref, index, frame):
    shard = frame.shape[0]
    column = lax.broadcasted_iota(jnp.int32, (1, CELLS), 1) % W
    zero = jnp.zeros_like(frame)
    ref[(*index, pl.ds(0, shard))] = jnp.where(column > 0, pltpu.roll(frame, 1, 1), zero)
    ref[(*index, pl.ds(shard, shard))] = frame
    ref[(*index, pl.ds(2 * shard, shard))] = jnp.where(
        column < W - 1, pltpu.roll(frame, CELLS - 1, 1), zero
    )


def row_taps(pieces, inputs, time_taps):
    weights = []
    for a in range(3):
        for block in range(PIECES):
            row = [
                part[block][9 * k + 3 * a + b] for part in pieces for k in time_taps for b in range(3)
            ]
            weights.append(jnp.concatenate(row, axis=1))
    product = jnp.dot(
        jnp.concatenate(weights, axis=0),
        jnp.concatenate(inputs, axis=0),
        preferred_element_type=jnp.float32,
    )
    own = product.shape[0] // 3
    cell = lax.broadcasted_iota(jnp.int32, (1, CELLS), 1)
    up = pltpu.roll(product[:own], W, 1)
    down = pltpu.roll(product[2 * own :], CELLS - W, 1)
    return (
        jnp.where(cell >= W, up, 0.0)
        + product[own : 2 * own]
        + jnp.where(cell < CELLS - W, down, 0.0)
    )


def conv_kernel(parts, slots_of, groups, *refs):
    refs = list(refs)
    clip_ref = refs.pop(0)
    frame_refs = [refs.pop(0) for _ in range(parts)]
    weight_refs = [refs.pop(0) for _ in range(1 if slots_of is None else PIECES)]
    sum_refs = [None if slots_of is None else refs.pop(0) for _ in groups]
    out_refs = [refs.pop(0) for _ in groups]
    shifted_ref = refs.pop(0)
    frame_count, shard, _ = frame_refs[0].shape
    own = out_refs[0].shape[1]
    first_frame = lax.axis_index("tm") * frame_count
    starts = piece_starts(own // PIECES)
    for p in range(parts):
        for f in range(0 if "own" in groups else frame_count // 2, frame_count):
            store_shifted(shifted_ref, (p, f), frame_refs[p][f])
        shifted_ref[p, frame_count] = jnp.zeros_like(shifted_ref[p, frame_count])

    def weight_rows(p, i):
        if slots_of is None:
            return weight_refs[0][:, pl.ds(starts[i], own // PIECES), :]
        return weight_refs[i][slots_of[p]]

    def convolved(j, time_taps):
        g = first_frame + j
        first = clip_start(clip_ref, g)
        inputs = []
        for p in range(parts):
            for k in time_taps:
                source = jnp.maximum(g - 2 + k, first) - first_frame
                source = jnp.where(source < 0, frame_count, jnp.minimum(source, frame_count))
                inputs.append(shifted_ref[p, source])
        pieces = [[weight_rows(p, i) for i in range(PIECES)] for p in range(parts)]
        return row_taps(pieces, inputs, time_taps)

    for group, out_ref, sum_ref in zip(groups, out_refs, sum_refs):
        if group == "next":
            for i, time_taps in enumerate(((0, 1), (0,))):
                total = convolved(frame_count + i, time_taps)
                if sum_ref is not None:
                    total = total + sum_ref[i]
                if groups == ("next",):
                    store_in_order(out_ref.at[i], total)
                else:
                    out_ref[i] = total
            continue

        for j in range(frame_count):
            total = convolved(j, (0, 1, 2))
            out_ref[j] = total if sum_ref is None else total + sum_ref[j]


def conv_parts(clip_lengths, shards_in, weights, slots_of, groups, sums=()):
    frame_count, shard, cells = shards_in[0].shape
    own, parts = shard, len(shards_in)
    vectors = pl.BlockSpec(memory_space=pltpu.VMEM)
    operands = [clip_lengths, *shards_in, *weights, *sums]
    frames = {"own": frame_count, "next": frame_count // 2}
    return pl.pallas_call(
        functools.partial(conv_kernel, parts, slots_of, groups),
        out_shape=[
            jax.ShapeDtypeStruct((frames[group], own, cells), jnp.float32) for group in groups
        ],
        in_specs=[pl.BlockSpec(memory_space=pltpu.SMEM)] + [vectors] * (len(operands) - 1),
        out_specs=[vectors] * len(groups),
        scratch_shapes=[pltpu.VMEM((parts, frame_count + 1, 3 * shard, cells), jnp.bfloat16)],
        compiler_params=pltpu.CompilerParams(vmem_limit_bytes=VMEM_BYTES),
        cost_estimate=pl.CostEstimate(flops=1024, bytes_accessed=1024, transcendentals=0),
        name="conv_parts",
    )(*operands)


def shift_kernel(*refs):
    *pair_refs, out_ref = refs
    half = pair_refs[0].shape[0]
    for i, pair_ref in enumerate(pair_refs):
        for f in range(half):
            store_shifted(out_ref, (i * half + f,), pair_ref[f])


def shifted_frames(*pairs):
    half, shard, cells = pairs[0].shape
    return pl.pallas_call(
        shift_kernel,
        out_shape=jax.ShapeDtypeStruct((len(pairs) * half, 3 * shard, cells), jnp.bfloat16),
        in_specs=[pl.BlockSpec(memory_space=pltpu.VMEM)] * len(pairs),
        out_specs=pl.BlockSpec(memory_space=pltpu.VMEM),
        compiler_params=pltpu.CompilerParams(vmem_limit_bytes=VMEM_BYTES),
        cost_estimate=pl.CostEstimate(flops=1500000000, bytes_accessed=1024, transcendentals=0),
        name="shifted_frames",
    )(*pairs)


def last_kernel(slot, far, *refs):
    refs = list(refs)
    clip_ref, shifted_ref = refs[:2]
    weight_refs = refs[2 : 2 + PIECES]
    sum_ref, arrived_ref, residual_ref, gain_ref, bias_ref = refs[2 + PIECES : 7 + PIECES]
    out_ref, total_ref = refs[7 + PIECES :]
    frame_count, half = residual_ref.shape[0], arrived_ref.shape[0]
    slab = lax.axis_index("tm")
    first_frame = slab * frame_count
    tail = (slab % 2 == 1) if far else (slab % 2 == 0)
    gain, bias = as_column(gain_ref[...]), as_column(bias_ref[...])

    for i in range(half):
        j = jnp.where(tail, i + half, i)
        g = first_frame + j
        first = clip_start(clip_ref, g)
        inputs = []
        for k in range(3):
            source = jnp.maximum(g - 2 + k, first) - first_frame
            inputs.append(shifted_ref[jnp.where(source < 0, source + frame_count + half, source)])
        pieces = [[ref[min(slot, ref.shape[0] - 1)] for ref in weight_refs]]
        total = row_taps(pieces, inputs, (0, 1, 2)) + sum_ref[j]
        store_in_order(total_ref.at[i], total)
        total = total_ref[i] + jnp.where(tail, 0.0, arrived_ref[i])
        out_ref[i] = finished(total, gain, bias, residual_ref[j])


def last_part(clip_lengths, far, slot, *operands):
    half, shard, cells = operands[2 + PIECES].shape
    vectors = pl.BlockSpec(memory_space=pltpu.VMEM)
    return pl.pallas_call(
        functools.partial(last_kernel, slot, far),
        out_shape=jax.ShapeDtypeStruct((half, shard, cells), jnp.bfloat16),
        in_specs=[pl.BlockSpec(memory_space=pltpu.SMEM)] + [vectors] * len(operands),
        out_specs=vectors,
        scratch_shapes=[
            pltpu.VMEM((half, shard, cells), jnp.float32),
        ],
        compiler_params=pltpu.CompilerParams(vmem_limit_bytes=VMEM_BYTES),
        cost_estimate=pl.CostEstimate(flops=1024 if far else 1024, bytes_accessed=1024, transcendentals=0),
        name="last_part",
    )(clip_lengths, *operands)


def slot_of(bounds_ref, frame_count, position):
    first = lax.axis_index("tm") * frame_count - frame_count // 2
    return position + first - bounds_ref[0, 0], bounds_ref[0, 1] - bounds_ref[0, 0]


def near_position(place, half):
    odd = lax.axis_index("tm") % 2 == 1
    return jnp.where(odd, place * half, (3 - place) * half)


def window_kernel(bounds_ref, near_ref, far_ref, far_in_ref, out_ref):
    half = near_ref.shape[0]
    capacity = out_ref.shape[0]
    for place, pair in enumerate((near_ref, far_ref, far_in_ref), 1):
        for i in range(half):
            slot, size = slot_of(bounds_ref, 2 * half, near_position(place, half) + i)

            @pl.when((slot >= 0) & (slot < size))
            def _():
                out_ref[slot] = pair[i].astype(jnp.float32)

    for slot in range(capacity):

        @pl.when(slot >= size)
        def _():
            out_ref[slot] = jnp.zeros_like(out_ref[slot])


def slots_kernel(bounds_ref, window_ref, near_in_ref, out_ref, staged_ref, sent_sem):
    capacity, channels, _ = window_ref.shape
    half = near_in_ref.shape[0]
    position = near_position(0, half)
    slot, size = slot_of(bounds_ref, 2 * half, position)
    rows = 16
    copies = []
    for start in range(0, channels, rows):
        frames = [window_ref[w, start : start + rows, :] for w in range(capacity)]
        for i in range(half):
            frame = near_in_ref[i, start : start + rows, :].astype(jnp.float32)
            for w in range(capacity):
                frames[w] = jnp.where((slot + i == w) & (w < size), frame, frames[w])
        block = jnp.stack(frames)
        staged_ref[start : start + rows] = jnp.swapaxes(block, 0, 1).astype(jnp.bfloat16)
        if (start + rows) % STAGE == 0:
            part = pl.ds(start + rows - STAGE, STAGE)
            copies.append(
                pltpu.make_async_copy(
                    staged_ref.at[part], out_ref.at[part], sent_sem.at[start // STAGE]
                )
            )
            copies[-1].start()
    for copy in copies:
        copy.wait()


def slots(bounds, near_in, near, far, far_in):
    half, channels, cells = near.shape
    capacity = 4 * half
    scalars = pl.BlockSpec(memory_space=pltpu.SMEM)
    vectors = pl.BlockSpec(memory_space=pltpu.VMEM)
    window = pl.pallas_call(
        window_kernel,
        out_shape=jax.ShapeDtypeStruct((capacity, channels, cells), jnp.float32),
        in_specs=[scalars] + [vectors] * 3,
        out_specs=vectors,
        compiler_params=pltpu.CompilerParams(vmem_limit_bytes=VMEM_BYTES),
        cost_estimate=pl.CostEstimate(flops=1000000000, bytes_accessed=1024, transcendentals=0),
        name="window",
    )(bounds, near, far, far_in)
    return pl.pallas_call(
        slots_kernel,
        out_shape=jax.ShapeDtypeStruct((channels, capacity, cells), jnp.bfloat16),
        in_specs=[scalars] + [vectors] * 2,
        out_specs=pl.BlockSpec(memory_space=pl.ANY),
        scratch_shapes=[
            pltpu.VMEM((channels, capacity, cells), jnp.bfloat16),
            pltpu.SemaphoreType.DMA((channels // STAGE,)),
        ],
        compiler_params=pltpu.CompilerParams(vmem_limit_bytes=VMEM_BYTES),
        name="slots",
    )(bounds, window, near_in)


def xor_permute(array, axis, bits):
    return lax.ppermute(array, axis, [(i, i ^ bits) for i in range(lax.axis_size(axis))])


def weight_blocks(by_tap):
    _, out_channels, shard = by_tap.shape
    chan_count = lax.axis_size("chan")
    own = out_channels // chan_count
    piece_rows = own // PIECES
    piece = lax.axis_index("tm") % PIECES
    me = lax.axis_index("chan")
    pieces = [
        lax.dynamic_slice(
            by_tap,
            (0, jnp.bitwise_xor(me, s) * own + piece * piece_rows, 0),
            (TAPS, piece_rows, shard),
        )
        for s in range(1, chan_count)
    ]
    return lax.dynamic_slice(by_tap, (0, me * own, 0), (TAPS, own, shard)), pieces


def shards(latents, conv_weight, norm_gain, norm_bias, clip_lengths, slab_bounds):
    own, frame_count, cells = latents.shape
    out_channels, _, _, shard = conv_weight.shape
    tm_count = lax.axis_size("tm")

    by_tap = jnp.transpose(conv_weight, (1, 2, 0, 3)).reshape(TAPS, out_channels, shard)
    own_weights, blocks = weight_blocks(by_tap)
    blocks, latents = lax.optimization_barrier((blocks, latents))
    by_frame = jnp.transpose(latents, (1, 0, 2))
    swapped = [xor_permute(block, "chan", s) for s, block in enumerate(blocks, 1)]

    half = frame_count // 2
    swapped[0], by_frame = lax.optimization_barrier((swapped[0], by_frame))
    first = xor_permute(by_frame, "chan", 1)
    swapped, kept = lax.optimization_barrier((jnp.stack(swapped), by_frame))
    second = xor_permute(kept, "chan", 2)
    total, following = conv_parts(clip_lengths, [by_frame], [own_weights], None, ("own", "next"))
    same_core = [swapped] + [xor_permute(swapped, "tm", bits) for bits in range(2, PIECES, 2)]
    same_core, total, first = lax.optimization_barrier((same_core, total, first))
    other_core = [xor_permute(piece, "tm", 1) for piece in same_core]
    weights = [piece for pair in zip(same_core, other_core) for piece in pair]
    third_tail = xor_permute(second[half:], "chan", 1)
    third_tail, second_head = lax.optimization_barrier((third_tail, second[:half]))
    third_head = xor_permute(second_head, "chan", 1)
    pair, slots_of = [first, second], (0, 1)
    (following,) = conv_parts(clip_lengths, pair, weights, slots_of, ("next",), [following])
    arrived = lax.ppermute(following, "tm", [(i, i + 1) for i in range(tm_count - 1)])
    halo = lax.ppermute(third_tail, "tm", [(i, i + 1) for i in range(tm_count - 1)])
    (total,) = conv_parts(clip_lengths, pair, weights, slots_of, ("own",), [total])
    operands = [shifted_frames(third_head, third_tail, halo), *weights, total]
    params = (by_frame, norm_gain.reshape(1, own), norm_bias.reshape(1, own))

    def swapped_pairs(start):
        pairs = range(start, tm_count - 1, 2)
        return [(i, i + 1) for i in pairs] + [(i + 1, i) for i in pairs]

    far = last_part(clip_lengths, True, 2, *operands, arrived, *params)
    far_in = lax.ppermute(far, "tm", swapped_pairs(1))
    arrived, far = lax.optimization_barrier((arrived, far))
    near = last_part(clip_lengths, False, 2, *operands, arrived, *params)
    near_in = lax.ppermute(near, "tm", swapped_pairs(0))
    return slots(slab_bounds, near_in, near, far, far_in)


def solution(mesh):
    placed = (
        P("chan", "tm", None),
        P(None, None, None, "chan"),
        P("chan"),
        P("chan"),
        P(),
        P("tm", None),
    )
    return jax.shard_map(
        shards, mesh=mesh, in_specs=placed, out_specs=P("chan", "tm", None), check_vma=False
    )
```

```python
import functools

import jax
import jax.numpy as jnp
from jax import lax
from jax.experimental import pallas as pl
from jax.experimental.pallas import tpu as pltpu
from jax.sharding import PartitionSpec as P

C = 512
GROUPS = 32
H = 16
W = 32
CELLS = H * W
GROUP_WIDTH = C // GROUPS
PIECES = 8
TAPS = 27
LANES = 128
STAGE = 32
VMEM_BYTES = 9 * 1024 * 1024

norm_eps = 1e-06


def clip_start(clip_ref, g):
    first = jnp.int32(0)
    running = jnp.int32(0)
    for c in range(clip_ref.shape[0]):
        first = jnp.where(running <= g, jnp.maximum(first, running), first)
        running = running + clip_ref[c]
    return first


def group_sum(grouped):
    tiles = [grouped[:, :, i : i + LANES] for i in range(0, CELLS, LANES)]
    while len(tiles) > 1:
        tiles = [x + y for x, y in zip(tiles[::2], tiles[1::2])]
    folded = tiles[0][:, :8] + tiles[0][:, 8:]
    return jnp.sum(jnp.sum(folded, axis=1, keepdims=True), axis=2, keepdims=True)


def group_norm(total, gain, bias):
    own = total.shape[0]
    grouped = total.reshape(own // GROUP_WIDTH, GROUP_WIDTH, CELLS)
    scale = 1.0 / (GROUP_WIDTH * CELLS)
    centred = grouped - group_sum(grouped) * scale
    variance = group_sum(centred * centred) * scale
    normed = (centred * lax.rsqrt(variance + norm_eps)).reshape(own, CELLS)
    return normed * gain + bias


def as_column(row):
    count = row.shape[1]
    return jnp.transpose(jnp.broadcast_to(row, (count, count)))[:, :1]


def finished(total, gain, bias, residual):
    normed = group_norm(total, gain, bias)
    activated = normed / (1.0 + jnp.exp(-normed))
    return (activated + residual.astype(jnp.float32)).astype(jnp.bfloat16)


def piece_starts(piece_rows):
    place = lax.axis_index("tm") % PIECES
    return [
        pl.multiple_of(jnp.bitwise_xor(place, i) * piece_rows, piece_rows) for i in range(PIECES)
    ]


def store_in_order(ref, total):
    rows = total.shape[0] // PIECES
    for block, start in enumerate(piece_starts(rows)):
        ref[pl.ds(start, rows), :] = total[block * rows : (block + 1) * rows]


def store_shifted(ref, index, frame):
    shard = frame.shape[0]
    column = lax.broadcasted_iota(jnp.int32, (1, CELLS), 1) % W
    zero = jnp.zeros_like(frame)
    ref[(*index, pl.ds(0, shard))] = jnp.where(column > 0, pltpu.roll(frame, 1, 1), zero)
    ref[(*index, pl.ds(shard, shard))] = frame
    ref[(*index, pl.ds(2 * shard, shard))] = jnp.where(
        column < W - 1, pltpu.roll(frame, CELLS - 1, 1), zero
    )


def row_taps(pieces, inputs, time_taps):
    weights = []
    for a in range(3):
        for block in range(PIECES):
            row = [
                part[block][9 * k + 3 * a + b] for part in pieces for k in time_taps for b in range(3)
            ]
            weights.append(jnp.concatenate(row, axis=1))
    product = jnp.dot(
        jnp.concatenate(weights, axis=0),
        jnp.concatenate(inputs, axis=0),
        preferred_element_type=jnp.float32,
    )
    own = product.shape[0] // 3
    cell = lax.broadcasted_iota(jnp.int32, (1, CELLS), 1)
    up = pltpu.roll(product[:own], W, 1)
    down = pltpu.roll(product[2 * own :], CELLS - W, 1)
    return (
        jnp.where(cell >= W, up, 0.0)
        + product[own : 2 * own]
        + jnp.where(cell < CELLS - W, down, 0.0)
    )


def conv_kernel(parts, slots_of, groups, *refs):
    refs = list(refs)
    clip_ref = refs.pop(0)
    frame_refs = [refs.pop(0) for _ in range(parts)]
    weight_refs = [refs.pop(0) for _ in range(1 if slots_of is None else PIECES)]
    sum_refs = [None if slots_of is None else refs.pop(0) for _ in groups]
    out_refs = [refs.pop(0) for _ in groups]
    shifted_ref = refs.pop(0)
    frame_count, shard, _ = frame_refs[0].shape
    own = out_refs[0].shape[1]
    first_frame = lax.axis_index("tm") * frame_count
    starts = piece_starts(own // PIECES)
    for p in range(parts):
        for f in range(0 if "own" in groups else frame_count // 2, frame_count):
            store_shifted(shifted_ref, (p, f), frame_refs[p][f])
        shifted_ref[p, frame_count] = jnp.zeros_like(shifted_ref[p, frame_count])

    def weight_rows(p, i):
        if slots_of is None:
            return weight_refs[0][:, pl.ds(starts[i], own // PIECES), :]
        return weight_refs[i][slots_of[p]]

    def convolved(j, time_taps):
        g = first_frame + j
        first = clip_start(clip_ref, g)
        inputs = []
        for p in range(parts):
            for k in time_taps:
                source = jnp.maximum(g - 2 + k, first) - first_frame
                source = jnp.where(source < 0, frame_count, jnp.minimum(source, frame_count))
                inputs.append(shifted_ref[p, source])
        pieces = [[weight_rows(p, i) for i in range(PIECES)] for p in range(parts)]
        return row_taps(pieces, inputs, time_taps)

    for group, out_ref, sum_ref in zip(groups, out_refs, sum_refs):
        if group == "next":
            for i, time_taps in enumerate(((0, 1), (0,))):
                total = convolved(frame_count + i, time_taps)
                if sum_ref is not None:
                    total = total + sum_ref[i]
                if groups == ("next",):
                    store_in_order(out_ref.at[i], total)
                else:
                    out_ref[i] = total
            continue

        for j in range(frame_count):
            total = convolved(j, (0, 1, 2))
            out_ref[j] = total if sum_ref is None else total + sum_ref[j]


def conv_parts(clip_lengths, shards_in, weights, slots_of, groups, sums=()):
    frame_count, shard, cells = shards_in[0].shape
    own, parts = shard, len(shards_in)
    vectors = pl.BlockSpec(memory_space=pltpu.VMEM)
    operands = [clip_lengths, *shards_in, *weights, *sums]
    frames = {"own": frame_count, "next": frame_count // 2}
    return pl.pallas_call(
        functools.partial(conv_kernel, parts, slots_of, groups),
        out_shape=[
            jax.ShapeDtypeStruct((frames[group], own, cells), jnp.float32) for group in groups
        ],
        in_specs=[pl.BlockSpec(memory_space=pltpu.SMEM)] + [vectors] * (len(operands) - 1),
        out_specs=[vectors] * len(groups),
        scratch_shapes=[pltpu.VMEM((parts, frame_count + 1, 3 * shard, cells), jnp.bfloat16)],
        compiler_params=pltpu.CompilerParams(vmem_limit_bytes=VMEM_BYTES),
        cost_estimate=pl.CostEstimate(flops=1024, bytes_accessed=1024, transcendentals=0),
        name="conv_parts",
    )(*operands)


def shift_kernel(*refs):
    *pair_refs, out_ref = refs
    half = pair_refs[0].shape[0]
    for i, pair_ref in enumerate(pair_refs):
        for f in range(half):
            store_shifted(out_ref, (i * half + f,), pair_ref[f])


def shifted_frames(*pairs):
    half, shard, cells = pairs[0].shape
    return pl.pallas_call(
        shift_kernel,
        out_shape=jax.ShapeDtypeStruct((len(pairs) * half, 3 * shard, cells), jnp.bfloat16),
        in_specs=[pl.BlockSpec(memory_space=pltpu.VMEM)] * len(pairs),
        out_specs=pl.BlockSpec(memory_space=pltpu.VMEM),
        compiler_params=pltpu.CompilerParams(vmem_limit_bytes=VMEM_BYTES),
        cost_estimate=pl.CostEstimate(flops=1500000000, bytes_accessed=1024, transcendentals=0),
        name="shifted_frames",
    )(*pairs)


def last_kernel(slot, far, *refs):
    refs = list(refs)
    clip_ref, shifted_ref = refs[:2]
    weight_refs = refs[2 : 2 + PIECES]
    sum_ref, arrived_ref, residual_ref, gain_ref, bias_ref = refs[2 + PIECES : 7 + PIECES]
    out_ref, total_ref = refs[7 + PIECES :]
    frame_count, half = residual_ref.shape[0], arrived_ref.shape[0]
    slab = lax.axis_index("tm")
    first_frame = slab * frame_count
    tail = (slab % 2 == 1) if far else (slab % 2 == 0)
    gain, bias = as_column(gain_ref[...]), as_column(bias_ref[...])

    for i in range(half):
        j = jnp.where(tail, i + half, i)
        g = first_frame + j
        first = clip_start(clip_ref, g)
        inputs = []
        for k in range(3):
            source = jnp.maximum(g - 2 + k, first) - first_frame
            inputs.append(shifted_ref[jnp.where(source < 0, source + frame_count + half, source)])
        pieces = [[ref[min(slot, ref.shape[0] - 1)] for ref in weight_refs]]
        total = row_taps(pieces, inputs, (0, 1, 2)) + sum_ref[j]
        store_in_order(total_ref.at[i], total)
        total = total_ref[i] + jnp.where(tail, 0.0, arrived_ref[i])
        out_ref[i] = finished(total, gain, bias, residual_ref[j])


def last_part(clip_lengths, far, slot, *operands):
    half, shard, cells = operands[2 + PIECES].shape
    vectors = pl.BlockSpec(memory_space=pltpu.VMEM)
    return pl.pallas_call(
        functools.partial(last_kernel, slot, far),
        out_shape=jax.ShapeDtypeStruct((half, shard, cells), jnp.bfloat16),
        in_specs=[pl.BlockSpec(memory_space=pltpu.SMEM)] + [vectors] * len(operands),
        out_specs=vectors,
        scratch_shapes=[
            pltpu.VMEM((half, shard, cells), jnp.float32),
        ],
        compiler_params=pltpu.CompilerParams(vmem_limit_bytes=VMEM_BYTES),
        cost_estimate=pl.CostEstimate(flops=1024 if far else 1024, bytes_accessed=1024, transcendentals=0),
        name="last_part",
    )(clip_lengths, *operands)


def slot_of(bounds_ref, frame_count, position):
    first = lax.axis_index("tm") * frame_count - frame_count // 2
    return position + first - bounds_ref[0, 0], bounds_ref[0, 1] - bounds_ref[0, 0]


def near_position(place, half):
    odd = lax.axis_index("tm") % 2 == 1
    return jnp.where(odd, place * half, (3 - place) * half)


def window_kernel(bounds_ref, near_ref, far_ref, far_in_ref, out_ref):
    half = near_ref.shape[0]
    capacity = out_ref.shape[0]
    for place, pair in enumerate((near_ref, far_ref, far_in_ref), 1):
        for i in range(half):
            slot, size = slot_of(bounds_ref, 2 * half, near_position(place, half) + i)

            @pl.when((slot >= 0) & (slot < size))
            def _():
                out_ref[slot] = pair[i]

    for slot in range(capacity):

        @pl.when(slot >= size)
        def _():
            out_ref[slot] = jnp.zeros_like(out_ref[slot])


def slots_kernel(bounds_ref, window_ref, near_in_ref, out_ref, staged_ref, sent_sem):
    capacity, channels, _ = window_ref.shape
    half = near_in_ref.shape[0]
    position = near_position(0, half)
    slot, size = slot_of(bounds_ref, 2 * half, position)
    rows = 16
    copies = []
    for start in range(0, channels, rows):
        frames = [
            window_ref[w, start : start + rows, :].astype(jnp.float32) for w in range(capacity)
        ]
        for i in range(half):
            frame = near_in_ref[i, start : start + rows, :].astype(jnp.float32)
            for w in range(capacity):
                frames[w] = jnp.where((slot + i == w) & (w < size), frame, frames[w])
        block = jnp.stack(frames)
        staged_ref[start : start + rows] = jnp.swapaxes(block, 0, 1).astype(jnp.bfloat16)
        if (start + rows) % STAGE == 0:
            part = pl.ds(start + rows - STAGE, STAGE)
            copies.append(
                pltpu.make_async_copy(
                    staged_ref.at[part], out_ref.at[part], sent_sem.at[start // STAGE]
                )
            )
            copies[-1].start()
    for copy in copies:
        copy.wait()


def slots(bounds, near_in, near, far, far_in):
    half, channels, cells = near.shape
    capacity = 4 * half
    scalars = pl.BlockSpec(memory_space=pltpu.SMEM)
    vectors = pl.BlockSpec(memory_space=pltpu.VMEM)
    window = pl.pallas_call(
        window_kernel,
        out_shape=jax.ShapeDtypeStruct((capacity, channels, cells), jnp.bfloat16),
        in_specs=[scalars] + [vectors] * 3,
        out_specs=vectors,
        compiler_params=pltpu.CompilerParams(vmem_limit_bytes=VMEM_BYTES),
        cost_estimate=pl.CostEstimate(flops=1000000000, bytes_accessed=1024, transcendentals=0),
        name="window",
    )(bounds, near, far, far_in)
    return pl.pallas_call(
        slots_kernel,
        out_shape=jax.ShapeDtypeStruct((channels, capacity, cells), jnp.bfloat16),
        in_specs=[scalars] + [vectors] * 2,
        out_specs=pl.BlockSpec(memory_space=pl.ANY),
        scratch_shapes=[
            pltpu.VMEM((channels, capacity, cells), jnp.bfloat16),
            pltpu.SemaphoreType.DMA((channels // STAGE,)),
        ],
        compiler_params=pltpu.CompilerParams(vmem_limit_bytes=VMEM_BYTES),
        name="slots",
    )(bounds, window, near_in)


def xor_permute(array, axis, bits):
    return lax.ppermute(array, axis, [(i, i ^ bits) for i in range(lax.axis_size(axis))])


def weight_blocks(by_tap):
    _, out_channels, shard = by_tap.shape
    chan_count = lax.axis_size("chan")
    own = out_channels // chan_count
    piece_rows = own // PIECES
    piece = lax.axis_index("tm") % PIECES
    me = lax.axis_index("chan")
    pieces = [
        lax.dynamic_slice(
            by_tap,
            (0, jnp.bitwise_xor(me, s) * own + piece * piece_rows, 0),
            (TAPS, piece_rows, shard),
        )
        for s in range(1, chan_count)
    ]
    return lax.dynamic_slice(by_tap, (0, me * own, 0), (TAPS, own, shard)), pieces


def shards(latents, conv_weight, norm_gain, norm_bias, clip_lengths, slab_bounds):
    own, frame_count, cells = latents.shape
    out_channels, _, _, shard = conv_weight.shape
    tm_count = lax.axis_size("tm")

    by_tap = jnp.transpose(conv_weight, (1, 2, 0, 3)).reshape(TAPS, out_channels, shard)
    own_weights, blocks = weight_blocks(by_tap)
    blocks, latents = lax.optimization_barrier((blocks, latents))
    by_frame = jnp.transpose(latents, (1, 0, 2))
    swapped = [xor_permute(block, "chan", s) for s, block in enumerate(blocks, 1)]

    half = frame_count // 2
    swapped[0], by_frame = lax.optimization_barrier((swapped[0], by_frame))
    first = xor_permute(by_frame, "chan", 1)
    swapped, kept = lax.optimization_barrier((jnp.stack(swapped), by_frame))
    second = xor_permute(kept, "chan", 2)
    total, following = conv_parts(clip_lengths, [by_frame], [own_weights], None, ("own", "next"))
    same_core = [swapped] + [xor_permute(swapped, "tm", bits) for bits in range(2, PIECES, 2)]
    same_core, total, first = lax.optimization_barrier((same_core, total, first))
    other_core = [xor_permute(piece, "tm", 1) for piece in same_core]
    weights = [piece for pair in zip(same_core, other_core) for piece in pair]
    third_tail = xor_permute(second[half:], "chan", 1)
    third_tail, second_head = lax.optimization_barrier((third_tail, second[:half]))
    third_head = xor_permute(second_head, "chan", 1)
    pair, slots_of = [first, second], (0, 1)
    (following,) = conv_parts(clip_lengths, pair, weights, slots_of, ("next",), [following])
    arrived = lax.ppermute(following, "tm", [(i, i + 1) for i in range(tm_count - 1)])
    halo = lax.ppermute(third_tail, "tm", [(i, i + 1) for i in range(tm_count - 1)])
    (total,) = conv_parts(clip_lengths, pair, weights, slots_of, ("own",), [total])
    operands = [shifted_frames(third_head, third_tail, halo), *weights, total]
    params = (by_frame, norm_gain.reshape(1, own), norm_bias.reshape(1, own))

    def swapped_pairs(start):
        pairs = range(start, tm_count - 1, 2)
        return [(i, i + 1) for i in pairs] + [(i + 1, i) for i in pairs]

    far = last_part(clip_lengths, True, 2, *operands, arrived, *params)
    far_in = lax.ppermute(far, "tm", swapped_pairs(1))
    arrived, far = lax.optimization_barrier((arrived, far))
    near = last_part(clip_lengths, False, 2, *operands, arrived, *params)
    near_in = lax.ppermute(near, "tm", swapped_pairs(0))
    return slots(slab_bounds, near_in, near, far, far_in)


def solution(mesh):
    placed = (
        P("chan", "tm", None),
        P(None, None, None, "chan"),
        P("chan"),
        P("chan"),
        P(),
        P("tm", None),
    )
    return jax.shard_map(
        shards, mesh=mesh, in_specs=placed, out_specs=P("chan", "tm", None), check_vma=False
    )
```
